32 devices in a mesh: fsdp: 32 (over z, y, x, core).
Axes of the slice: x: 2, y: 2, z: 4, core: 2. Of those that a mesh axis runs over, the one named last changes fastest.
Arguments:
- tokens: bfloat16 [16384, 1024], P('fsdp'), may hold values from -12 to 12
- cotangent: bfloat16 [16384, 1024], P('fsdp'), may hold values from -6 to 6
- seq_lengths: int32 [64, 4], P('fsdp'), may hold values from 1 to 192, 256 in all within a row
- routes: int32 [16384, 8], P('fsdp'), may hold values from 0 to 15, as said below
- attn_gain: bfloat16 [1024], P('fsdp'), may hold values from 0.099609375 to 1.8984375
- w_query: bfloat16 [1024, 1024], P('fsdp'), may hold values from -0.1875 to 0.1875
- w_keyval: bfloat16 [1024, 1024], P('fsdp'), may hold values from -0.1875 to 0.1875
- w_out: bfloat16 [1024, 1024], P('fsdp'), may hold values from -0.75 to 0.75
- moe_gain: bfloat16 [1024], P('fsdp'), may hold values from 0.099609375 to 1.8984375
- w_router: bfloat16 [1024, 16], P('fsdp'), may hold values from -0.125 to 0.125
- w_gateup: bfloat16 [16, 1024, 1024], P(None, 'fsdp'), may hold values from -0.1875 to 0.1875
- w_down: bfloat16 [16, 512, 1024], P(None, 'fsdp'), may hold values from -0.5 to 0.5
Outputs:
- output: bfloat16 [16384, 1024], P('fsdp')
- grad_tokens: float32 [16384, 1024], P('fsdp')
- grad_attn_gain: float32 [1024], P('fsdp')
- grad_query: float32 [1024, 1024], P('fsdp')
- grad_keyval: float32 [1024, 1024], P('fsdp')
- grad_out: float32 [1024, 1024], P('fsdp')
- grad_moe_gain: float32 [1024], P('fsdp')
- grad_router: float32 [1024, 16], P('fsdp')
- grad_gateup: float32 [16, 1024, 1024], P(None, 'fsdp')
- grad_down: float32 [16, 512, 1024], P(None, 'fsdp')
The draws below stay inside these ranges and needn't reach their ends.
Inputs may be any that keep to these rules, and one draw needn't show every extreme that they name: `seq_lengths`: row b holds, in order, the lengths of the 4 sequences that fill rows b * 256 to (b + 1) * 256 - 1 of the tokens; they sum to 256. `routes`: the 8 entries of a row differ; within each aligned block of 256 rows (one micro-batch of one device), 8 experts, which ones drawn afresh for each block, are named by exactly 192 rows each, and each of the other experts by exactly 64 rows.
All inputs are finite; a program needn't handle non-finite values.
Results may differ from the reference program's by a relative error of at most 0.014.
Values may be sent and summed in bfloat16 or wider, within the bound.
No kernel may reach another device: no remote copies, remote signals or barrier semaphores. Data moves between devices by JAX's collectives and lax.ppermute only.
A program may use at most 256 MiB of HBM per device.

```python
import math
import jax
import jax.numpy as jnp
import numpy as np
from jax import lax

D = 1024
H = 16
KV = 8
HD = 64
FF = 512
TOPK = 8
E = 16
SEQS = 4
MB = 256
MOST = 192
TOKENS = 16384
BLOCKS = 64


def draw_routes(key, part):
    halves = E // 2
    heavy_pick = 3 * TOPK // 4
    light_pick = TOPK - heavy_pick
    row_index = jnp.arange(MB, dtype=jnp.int32)
    cycle_index = row_index % halves
    heavy_local = (cycle_index[:, None] + jnp.arange(heavy_pick, dtype=jnp.int32)[None, :]) % halves
    light_local = (cycle_index[:, None] + jnp.arange(light_pick, dtype=jnp.int32)[None, :]) % halves + halves
    pattern = jnp.concatenate([heavy_local, light_local], axis=1).astype(jnp.int32)
    base_key = jax.random.fold_in(key, 7919)

    def column_shuffle(sub_key):
        return jax.random.permutation(sub_key, TOPK).astype(jnp.int32)

    def one_block(block_index):
        block_key = jax.random.fold_in(base_key, block_index)
        expert_key, row_key, column_key = jax.random.split(block_key, 3)
        relabel = jax.random.permutation(expert_key, E).astype(jnp.int32)
        row_order = jax.random.permutation(row_key, MB).astype(jnp.int32)
        column_keys = jax.random.split(column_key, MB)
        column_order = jax.vmap(column_shuffle)(column_keys)
        shuffled = jnp.take_along_axis(pattern[row_order], column_order, axis=1)
        return relabel[shuffled].astype(jnp.int32)
    drawn = jax.vmap(one_block)(jnp.arange(BLOCKS, dtype=jnp.int32))
    return drawn.reshape(BLOCKS * MB, TOPK).astype(jnp.int32)


def with_spikes(entries, stream_key, source, target, shards_of, factor):
    def block_of(dim):
        return (jnp.arange(entries.shape[dim]) // (entries.shape[dim] // shards_of)).reshape((-1,) + (1,) * (entries.ndim - 1 - dim))

    one_side = jax.random.permutation(stream_key, shards_of)[block_of(target)]
    second = (block_of(target) + shards_of // 2) % shards_of
    return jnp.where((block_of(source) == one_side) | (block_of(source) == second), factor * entries, entries)


def levels(rng, shape, shards, low, top_value):
    def one(dim, parts):
        steps = jax.random.uniform(jax.random.fold_in(jax.random.fold_in(rng, 6), dim), (parts,), jnp.float32, low / len(shards), top_value / len(shards))
        return jnp.repeat(jnp.exp(steps), shape[dim] // parts).reshape((-1,) + (1,) * (len(shape) - dim - 1))

    factor_of = one(*shards[0])
    for cut in shards[1:]:
        factor_of = factor_of * one(*cut)
    return factor_of


def split_up(count, total, limit, skew):
    weights = [(1 << 20) // math.isqrt(rank ** skew) + 1 for rank in range(2, count + 1)]
    rest, given = total - limit - (count - 1), [1] * (count - 1)
    while rest > 0:
        movable = [i for i in range(count - 1) if given[i] < limit]
        mass, left = sum([weights[i] for i in movable]), rest
        for i in movable:
            more = min(limit - given[i], max(1, left * weights[i] // mass), rest)
            given[i] = given[i] + more
            rest = rest - more
    return np.array([limit] + given)


def ragged_sizes(stream_key, amount, total, reach, skew):
    if amount == 2:
        one = jax.random.randint(stream_key, (), max(1, total - reach), min(reach, total - 1) + 1)
        return jnp.stack([one, total - one])
    sizes = jnp.asarray(split_up(amount, total, reach, skew), jnp.int32)
    twos = (amount - 1) // 2
    source_of, sink = sizes[1:1 + 2 * twos:2], sizes[2:2 + 2 * twos:2]
    slack = jnp.minimum(source_of - 1, reach - sink)
    moved = jax.random.randint(jax.random.fold_in(stream_key, 1), (twos,), 0, 1 << 20) % (slack + 1)
    sizes = sizes.at[1:1 + 2 * twos:2].set(source_of - moved).at[2:2 + 2 * twos:2].set(sink + moved)
    return sizes[jax.random.permutation(jax.random.fold_in(stream_key, 2), amount)]


def normal_values(own_key, dims, deviation, most, cuts=(), kind=jnp.bfloat16):
    array = deviation * jax.random.normal(own_key, dims, jnp.float32)
    if cuts:
        array = array * levels(own_key, dims, cuts, -0.22, 0.18)
    return jnp.clip(array, -most, most).astype(kind)


def gaussian_with(stream_key, dims, scale, reach, pieces, heavy, held_as=jnp.bfloat16):
    values = scale * jax.random.normal(stream_key, dims, jnp.float32)
    if pieces:
        values = values * levels(stream_key, dims, pieces, -0.22, 0.18)
    return jnp.clip(with_spikes(values, jax.random.fold_in(stream_key, 3), *heavy), -reach, reach).astype(held_as)


def setup_inputs(seed: int = 0) -> dict:
    keys = jax.random.split(jax.random.key(seed), 13)
    tokens = gaussian_with(keys[0], (TOKENS, D), 1.0, 12.0, ((0, 32),), (0, 1, 32, 2.75))
    cotangent = normal_values(keys[1], (TOKENS, D), 1.0, 6.0, ((0, 32),))
    seq_lengths = jax.vmap(lambda own: ragged_sizes(own, SEQS, MB, MOST, 2))(jax.random.split(keys[2], BLOCKS)).reshape((BLOCKS, SEQS)).astype(jnp.int32)
    routes = draw_routes(jax.random.fold_in(keys[12], 71), 0)
    attn_gain = jnp.clip(1.0 + 0.18 * jax.random.normal(keys[4], (D,), jnp.float32), 0.099609375, 1.8984375).astype(jnp.bfloat16)
    w_query = normal_values(keys[5], (D, H * HD), D ** -0.5, 0.1875, ((0, 32),))
    w_keyval = normal_values(keys[6], (D, 2 * KV * HD), D ** -0.5, 0.1875, ((0, 32),))
    w_out = normal_values(keys[7], (H * HD, D), (H * HD // 16) ** -0.5, 0.75, ((0, 32),))
    moe_gain = jnp.clip(1.0 + 0.18 * jax.random.normal(keys[8], (D,), jnp.float32), 0.099609375, 1.8984375).astype(jnp.bfloat16)
    w_router = normal_values(keys[9], (D, E), (2 * D) ** -0.5, 0.125, ((0, 32),))
    w_gateup = normal_values(keys[10], (E, D, 2 * FF), D ** -0.5, 0.1875, ((1, 32),))
    w_down = normal_values(keys[11], (E, FF, D), (FF // 4) ** -0.5, 0.5, ((1, 32),))
    return {"tokens": tokens, "cotangent": cotangent, "seq_lengths": seq_lengths, "routes": routes, "attn_gain": attn_gain, "w_query": w_query, "w_keyval": w_keyval, "w_out": w_out, "moe_gain": moe_gain, "w_router": w_router, "w_gateup": w_gateup, "w_down": w_down}


@jax.custom_vjp
def low(v):
    return lax.optimization_barrier(v.astype(jnp.bfloat16)).astype(jnp.float32)

@jax.custom_vjp
def low_back(v):
    return v

def low_keep(v):
    return (low(v), None)

def low_pass(kept, grad):
    return (grad,)

def back_keep(v):
    return (v, None)

def back_low(kept, grad):
    return (low(grad),)
low.defvjp(low_keep, low_pass)
low_back.defvjp(back_keep, back_low)
EPS = 1e-05
HIGHEST = lax.Precision.HIGHEST

def rms_scale(values, gain):
    return values * lax.rsqrt(lax.optimization_barrier(jnp.mean(values * values, axis=-1, keepdims=True)) + EPS) * gain

def rotate(values, cosine, sine):
    half = values.shape[-1] // 2
    turned = jnp.concatenate([-values[..., half:], values[..., :half]], axis=-1)
    return values * cosine + turned * sine

def layout(lengths, count):
    ends = jnp.cumsum(lengths).astype(jnp.int32)
    index = jnp.arange(count, dtype=jnp.int32)
    segment = lax.optimization_barrier(jnp.sum((index[:, None] >= ends[None, :]).astype(jnp.int32), axis=1)).astype(jnp.int32)
    start = lax.optimization_barrier(jnp.max(jnp.where(ends[None, :] <= index[:, None], ends[None, :], 0), axis=1)).astype(jnp.int32)
    return (segment, index - start)

def rope_tables(position, width):
    freq = jnp.exp(-(jnp.arange(0, width, 2, dtype=jnp.float32) / width) * jnp.log(10000.0))
    angle = position.astype(jnp.float32)[:, None] * freq[None, :]
    angle = jnp.concatenate([angle, angle], axis=1)
    return (jnp.cos(angle)[:, None, :], jnp.sin(angle)[:, None, :])

def block_forward(rows_in, lengths, route, weights):
    gain_in, query_w, keyval_w, out_w, gain_mid, router_w, gateup_w, down_w = weights
    count = rows_in.shape[0]
    segment, position = layout(lengths, count)
    index = jnp.arange(count, dtype=jnp.int32)
    allowed = (segment[:, None] == segment[None, :]) & (index[None, :] <= index[:, None])
    cosine, sine = rope_tables(position, HD)
    normed_in = low(rms_scale(rows_in, gain_in))
    q_lin = low_back(jnp.dot(normed_in, query_w, precision=HIGHEST))
    kv_lin = low_back(jnp.dot(normed_in, keyval_w, precision=HIGHEST))
    query = low(rotate(q_lin.reshape(count, H, HD), cosine, sine)).reshape(count, KV, H // KV, HD)
    key = low(rotate(kv_lin[:, :KV * HD].reshape(count, KV, HD), cosine, sine))
    value = low(kv_lin[:, KV * HD:].reshape(count, KV, HD))
    score = low_back(jnp.einsum('igjd,ngd->gjin', query, key, precision=HIGHEST) * 0.125)
    score = jnp.where(allowed, score, -1e+30)
    weight = low(jax.nn.softmax(score, axis=-1))
    mixed = jnp.einsum('gjin,ngd->igjd', weight, value, precision=HIGHEST).reshape(count, H * HD)
    mixed = low(low_back(mixed))
    resid = rows_in + low_back(jnp.dot(mixed, out_w, precision=HIGHEST))
    normed_mid = low(rms_scale(resid, gain_mid))
    logits = low_back(jnp.dot(normed_mid, router_w, precision=HIGHEST))
    onehot = (route[:, :, None] == jnp.arange(E, dtype=jnp.int32)[None, None, :]).astype(jnp.float32)
    chosen = jnp.einsum('rke,re->rk', onehot, logits, precision=HIGHEST)
    gates = jax.nn.softmax(chosen, axis=-1)
    combine = jnp.einsum('rk,rke->re', gates, onehot, precision=HIGHEST)
    gateup = low_back(jnp.einsum('rd,edf->ref', normed_mid, gateup_w, precision=HIGHEST))
    act = low(jax.nn.silu(gateup[..., :FF]) * gateup[..., FF:])
    expert_out = low_back(jnp.einsum('ref,efd->red', act, down_w, precision=HIGHEST))
    return resid + jnp.einsum('re,red->rd', combine, expert_out, precision=HIGHEST)

def reference(tokens, cotangent, seq_lengths, routes, attn_gain, w_query, w_keyval, w_out, moe_gain, w_router, w_gateup, w_down):
    weights = (attn_gain.astype(jnp.float32), w_query.astype(jnp.float32), w_keyval.astype(jnp.float32), w_out.astype(jnp.float32), moe_gain.astype(jnp.float32), w_router.astype(jnp.float32), w_gateup.astype(jnp.float32), w_down.astype(jnp.float32))
    total_rows = tokens.shape[0]
    block_count = seq_lengths.shape[0]
    route_blocks = routes.reshape(block_count, MB, TOPK)

    def forward(rows_all, weight_set):
        blocks = rows_all.reshape(block_count, MB, D)
        stepper = jax.checkpoint(lambda item: block_forward(item[0], item[1], item[2], weight_set))
        return lax.map(stepper, (blocks, seq_lengths, route_blocks)).reshape(total_rows, D)
    result, pullback = jax.vjp(forward, tokens.astype(jnp.float32), weights)
    grad_in, grad_set = pullback(cotangent.astype(jnp.float32))
    return (result.astype(jnp.bfloat16), grad_in, grad_set[0], grad_set[1], grad_set[2], grad_set[3], grad_set[4], grad_set[5], grad_set[6], grad_set[7])
```

```python
import functools

import jax
import jax.numpy as jnp
from jax import lax
from jax.experimental import pallas as pl
from jax.experimental.pallas import tpu as pltpu
from jax.sharding import Mesh, PartitionSpec as P

D = 1024
HD = 64
FF = 512
E = 16
MB = 256
GROUPS = 8
PLANE = 8
OWN = E // PLANE
LANES = 128
WIDE = 3 * D + LANES
EPS = 1e-05
NEG = -1e30

BF = jnp.bfloat16
F32 = jnp.float32
PLANE_AXES = ("y", "x", "c")
ALL = ("z", "y", "x", "c")


def dot(a, b, ca=1, cb=0):
    return lax.dot_general(a, b, (((ca,), (cb,)), ((), ())), preferred_element_type=F32)


def mean_rows(v):
    return jnp.sum(v, axis=-1, keepdims=True) * (1.0 / v.shape[-1])


def lane_of(rows):
    return lax.broadcasted_iota(jnp.int32, (rows, LANES), 1)


def turned(t, low):
    return jnp.where(low, pltpu.roll(t, LANES - HD // 2, 1), pltpu.roll(t, HD // 2, 1))


def swap(t):
    return pltpu.roll(t, HD, 1)


def gain_rows(w_ref):
    cols = w_ref[:, 3 * D :].astype(F32).T
    return cols[E : E + 1, :], cols[E + 1 : E + 2, :]


def bias_of(lens_ref, micro):
    row = lax.broadcasted_iota(jnp.int32, (MB, MB), 0)
    col = lax.broadcasted_iota(jnp.int32, (MB, MB), 1)
    start = jnp.zeros((MB, MB), jnp.int32)
    end = jnp.int32(0)
    for s in range(3):
        end = end + lens_ref[micro, s]
        start = jnp.where(row >= end, end, start)
    return jnp.where((col >= start) & (col <= row), 0.0, NEG)


def split_pair(block, half):
    low = lane_of(block.shape[0]) < HD
    other = swap(block)
    here, there = (block, other) if half == 0 else (other, block)
    return jnp.concatenate(
        [jnp.where(low, here, 0.0), jnp.where(low, 0.0, there)], axis=0
    ).astype(BF)


def softmax_pair(score, bias):
    halves = []
    for h in range(2):
        s = score[:, h * MB : (h + 1) * MB] * 0.125 + bias
        e = jnp.exp(s - jnp.max(s, axis=1, keepdims=True))
        halves.append(e * (1.0 / jnp.sum(e, axis=1, keepdims=True)))
    return jnp.concatenate(halves, axis=1)


def attention_forward_kernel(lens_ref, tok_ref, w_ref, cos_ref, sin_ref, nm_ref, q_ref, kv_ref, mixed_ref, resid_ref):
    micro = pl.program_id(0)
    gain_in, gain_mid = gain_rows(w_ref)
    x = tok_ref[...].astype(F32)
    normed = (x * lax.rsqrt(mean_rows(x * x) + EPS) * gain_in).astype(BF)
    q_lin = dot(normed, w_ref[:, :D])
    kv_lin = dot(normed, w_ref[:, D : 2 * D])
    cosine, sine = cos_ref[...], sin_ref[...]
    low = (lane_of(MB) % HD) < HD // 2
    bias = bias_of(lens_ref, micro)
    mixed = []
    for pair in range(GROUPS // 2):
        lanes = slice(pair * LANES, (pair + 1) * LANES)
        k_pair = kv_lin[:, lanes]
        k_pair = k_pair * cosine + turned(k_pair, low) * sine
        v_pair = kv_lin[:, D // 2 + pair * LANES : D // 2 + (pair + 1) * LANES]
        kv_ref[:, lanes] = k_pair.astype(BF)
        kv_ref[:, D // 2 + pair * LANES : D // 2 + (pair + 1) * LANES] = v_pair.astype(BF)
        for half in range(2):
            group = 2 * pair + half
            q = q_lin[:, group * LANES : (group + 1) * LANES]
            q = (q * cosine + turned(q, low) * sine).astype(BF)
            q_ref[:, group * LANES : (group + 1) * LANES] = q
            score = dot(q, split_pair(k_pair, half), 1, 1)
            weight = softmax_pair(score, bias).astype(BF)
            mixed.append(dot(weight, split_pair(v_pair, half)).astype(BF))
    mixed = jnp.concatenate(mixed, axis=1)
    mixed_ref[...] = mixed
    resid = x + dot(mixed, w_ref[:, 2 * D : 3 * D])
    resid_ref[...] = resid
    nm_ref[...] = (resid * lax.rsqrt(mean_rows(resid * resid) + EPS) * gain_mid).astype(BF)


def masked_gates(logits, routed):
    top = jnp.max(jnp.where(routed, logits, NEG), axis=1, keepdims=True)
    e = jnp.where(routed, jnp.exp(jnp.minimum(logits - top, 0.0)), 0.0)
    return e * (1.0 / jnp.sum(e, axis=1, keepdims=True))


def expert_kernel(me_ref, nm_ref, cot_ref, wr_ref, *refs):
    weights = [(refs[2 * e], refs[2 * e + 1]) for e in range(OWN)]
    out_ref, dmid_ref, grad_ref, acc_gu, acc_dn = refs[2 * OWN :]
    step = pl.program_id(0)

    @pl.when(step == 0)
    def _():
        acc_gu[...] = jnp.zeros_like(acc_gu)
        acc_dn[...] = jnp.zeros_like(acc_dn)

    rows = nm_ref.shape[0]
    nm = nm_ref[...]
    cot = cot_ref[:, :D]
    lane = lane_of(rows)
    gates = masked_gates(dot(nm, wr_ref[...]), cot_ref[:, D:].astype(F32) > 0.5)
    out = jnp.zeros((rows, D), F32)
    d_mid = jnp.zeros((rows, D), F32)
    extra = jnp.zeros((rows, LANES), F32)
    for e in range(OWN):
        expert = me_ref[0] * OWN + e
        w_gu = weights[e][0][...].reshape(D, 2 * FF)
        w_dn = weights[e][1][...].reshape(FF, D)
        combine = jnp.sum(jnp.where(lane == expert, gates, 0.0), axis=1, keepdims=True)
        gateup = dot(nm, w_gu)
        gate, up = gateup[:, :FF], gateup[:, FF:]
        s = 1.0 / (1.0 + jnp.exp(-gate))
        silu = gate * s
        act = silu * up
        d_plain = dot(cot, w_dn, 1, 1)
        d_combine = jnp.sum(act * d_plain, axis=1, keepdims=True)
        act = (act * combine).astype(BF)
        out = out + dot(act, w_dn)
        d_act = d_plain * combine
        d_gateup = jnp.concatenate(
            [(d_act * up * (s * (1.0 + gate * (1.0 - s)))).astype(BF), (d_act * silu).astype(BF)], axis=1
        )
        d_mid = d_mid + dot(d_gateup, w_gu, 1, 1)
        acc_gu[e] += dot(nm, d_gateup, 0, 0)
        acc_dn[e] += dot(act, cot, 0, 0)
        high = d_combine.astype(BF).astype(F32)
        extra = extra + jnp.where(lane == expert, high, 0.0) + jnp.where(lane == expert + E, d_combine - high, 0.0)
    out_ref[...] = out.astype(BF)
    dmid_ref[:, :D] = d_mid.astype(BF)
    dmid_ref[:, D:] = extra.astype(BF)

    @pl.when(step == pl.num_programs(0) - 1)
    def _():
        outer = grad_ref.shape[1]
        up_rows, down_rows = D // outer, FF // outer
        for e in range(OWN):
            for z in range(outer):
                grad_ref[e, z, :up_rows] = acc_gu[e, z * up_rows : (z + 1) * up_rows].astype(BF)
                grad_ref[e, z, up_rows:] = acc_dn[e, z * down_rows : (z + 1) * down_rows].astype(BF)


def join_pair(a0, b0, a1, b1, low):
    return jnp.where(low, a0, b1) + swap(jnp.where(low, a1, b0))


def attention_backward_kernel(
    lens_ref, tok_ref, cot_ref, resid_ref, q_ref, kv_ref, mixed_ref, nm_ref, dmid_ref, w_ref, cos_ref, sin_ref,
    rows_ref, grad_ref, acc_ref, gain_ref,
):
    micro = pl.program_id(0)

    @pl.when(micro == 0)
    def _():
        acc_ref[...] = jnp.zeros_like(acc_ref)
        gain_ref[...] = jnp.zeros_like(gain_ref)

    gain_in, gain_mid = gain_rows(w_ref)
    lane = lane_of(MB)
    cot = cot_ref[:, :D].astype(F32)
    resid = resid_ref[...]
    nm = nm_ref[...]
    w_small = w_ref[:, 3 * D :]
    gates = masked_gates(dot(nm, w_small), cot_ref[:, D:].astype(F32) > 0.5)
    pieces = dmid_ref[:, D:].astype(F32)
    d_gates = pieces + pltpu.roll(pieces, LANES - E, 1)
    d_logits = gates * (d_gates - jnp.sum(gates * d_gates, axis=1, keepdims=True))
    d_logits = jnp.where(lane < E, d_logits, 0.0).astype(BF)
    acc_ref[:, 3 * D :] += dot(nm, d_logits, 0, 0)
    d_mid = dmid_ref[:, :D].astype(F32) + dot(d_logits, w_small, 1, 1)
    inverse = lax.rsqrt(mean_rows(resid * resid) + EPS)
    u = d_mid * gain_mid
    d_resid = cot + inverse * u - resid * (inverse * inverse * inverse) * mean_rows(u * resid)
    gain_ref[1:2, :] += jnp.sum(d_mid * resid * inverse, axis=0, keepdims=True)
    d_branch = d_resid.astype(BF)
    acc_ref[:, 2 * D : 3 * D] += dot(mixed_ref[...], d_branch, 0, 0)
    d_mixed = dot(d_branch, w_ref[:, 2 * D : 3 * D], 1, 1).astype(BF)

    cosine, sine = cos_ref[...], sin_ref[...]
    low = (lane % HD) < HD // 2
    head_low = lane < HD
    bias = bias_of(lens_ref, micro)
    d_q, d_k, d_v = [], [], []
    for pair in range(GROUPS // 2):
        k_pair = kv_ref[:, pair * LANES : (pair + 1) * LANES].astype(F32)
        v_pair = kv_ref[:, D // 2 + pair * LANES : D // 2 + (pair + 1) * LANES].astype(F32)
        keys, values = [], []
        for half in range(2):
            group = 2 * pair + half
            q = q_ref[:, group * LANES : (group + 1) * LANES]
            dm = d_mixed[:, group * LANES : (group + 1) * LANES]
            k_two = split_pair(k_pair, half)
            p = softmax_pair(dot(q, k_two, 1, 1), bias)
            d_weight = dot(dm, split_pair(v_pair, half), 1, 1)
            scored = p * d_weight
            d_score = []
            for h in range(2):
                part = slice(h * MB, (h + 1) * MB)
                total = jnp.sum(scored[:, part], axis=1, keepdims=True)
                d_score.append((p[:, part] * (d_weight[:, part] - total)).astype(BF))
            d_score = jnp.concatenate(d_score, axis=1)
            d_query = dot(d_score, k_two) * 0.125
            d_q.append((d_query * cosine - turned(d_query, low) * sine).astype(BF))
            d_key = dot(d_score, q, 0, 0) * 0.125
            d_value = dot(p.astype(BF), dm, 0, 0)
            keys += [d_key[:MB], d_key[MB:]]
            values += [d_value[:MB], d_value[MB:]]
        d_key = join_pair(*keys, head_low)
        d_k.append((d_key * cosine - turned(d_key, low) * sine).astype(BF))
        d_v.append(join_pair(*values, head_low).astype(BF))
    d_q = jnp.concatenate(d_q, axis=1)
    d_kv = jnp.concatenate(d_k + d_v, axis=1)

    x = tok_ref[...].astype(F32)
    inverse = lax.rsqrt(mean_rows(x * x) + EPS)
    normed = (x * inverse * gain_in).astype(BF)
    acc_ref[:, :D] += dot(normed, d_q, 0, 0)
    acc_ref[:, D : 2 * D] += dot(normed, d_kv, 0, 0)
    d_in = dot(d_q, w_ref[:, :D], 1, 1) + dot(d_kv, w_ref[:, D : 2 * D], 1, 1)
    v = d_in * gain_in
    rows_ref[...] = d_resid + inverse * v - x * (inverse * inverse * inverse) * mean_rows(v * x)
    gain_ref[0:1, :] += jnp.sum(d_in * x * inverse, axis=0, keepdims=True)

    @pl.when(micro == pl.num_programs(0) - 1)
    def _():
        grad_ref[:, : 3 * D] = acc_ref[:, : 3 * D].astype(BF)
        gains = jnp.concatenate(
            [jnp.zeros((E, D), F32), gain_ref[...], jnp.zeros((LANES - E - gain_ref.shape[0], D), F32)], axis=0
        )
        grad_ref[:, 3 * D :] = (acc_ref[:, 3 * D :] + gains.T).astype(BF)


def blk(shape, index, buffers=None):
    if buffers is None:
        return pl.BlockSpec(shape, index)
    return pl.BlockSpec(shape, index, pipeline_mode=pl.Buffered(buffers))


def kernel_params(mib=58):
    return pltpu.CompilerParams(dimension_semantics=("arbitrary",), vmem_limit_bytes=mib << 20)


def rows_spec(width):
    return blk((MB, width), lambda i, *_: (i, 0))


def attention_forward(tokens, lengths, packed, cosine, sine):
    rows = tokens.shape[0]
    shape = jax.ShapeDtypeStruct
    return pl.pallas_call(
        attention_forward_kernel,
        grid_spec=pltpu.PrefetchScalarGridSpec(
            num_scalar_prefetch=1,
            grid=(rows // MB,),
            in_specs=[
                rows_spec(D),
                blk((D, WIDE), lambda i, *_: (0, 0), 1),
                rows_spec(LANES),
                rows_spec(LANES),
            ],
            out_specs=[rows_spec(D)] * 5,
        ),
        out_shape=[shape((rows, D), BF)] * 4 + [shape((rows, D), F32)],
        compiler_params=kernel_params(),
        name="attention_forward",
    )(lengths, tokens, packed, cosine, sine)


def experts(me, nm, cot, packed, homes, step_rows=512):
    rows = nm.shape[0]
    outer = homes[0].shape[0]
    up_rows, down_rows = D // outer, FF // outer
    shape = jax.ShapeDtypeStruct
    spec = lambda width: blk((step_rows, width), lambda i, *_: (i, 0))
    home_specs, home_args = [], []
    for home in homes:
        home_specs += [
            blk((outer, up_rows, D), lambda i, *_: (0, 0, 0), 1),
            blk((outer, down_rows, D), lambda i, *_: (0, 2, 0), 1),
        ]
        home_args += [home, home]
    return pl.pallas_call(
        expert_kernel,
        grid_spec=pltpu.PrefetchScalarGridSpec(
            num_scalar_prefetch=1,
            grid=(rows // step_rows,),
            in_specs=[spec(D), spec(D + LANES), blk((D, LANES), lambda i, *_: (0, 3 * D // LANES), 1)] + home_specs,
            out_specs=[
                spec(D),
                spec(D + LANES),
                blk((OWN, outer, up_rows + down_rows, D), lambda i, *_: (0, 0, 0, 0), 1),
            ],
            scratch_shapes=[pltpu.VMEM((OWN, D, 2 * FF), F32), pltpu.VMEM((OWN, FF, D), F32)],
        ),
        out_shape=[
            shape((rows, D), BF),
            shape((rows, D + LANES), BF),
            shape((OWN, outer, up_rows + down_rows, D), BF),
        ],
        compiler_params=kernel_params(),
        name="experts",
    )(me, nm, cot, packed, *home_args)


def attention_backward(tokens, lengths, cot, resid, q, kv, mixed, nm, d_mid, packed, cosine, sine):
    rows = tokens.shape[0]
    shape = jax.ShapeDtypeStruct
    return pl.pallas_call(
        attention_backward_kernel,
        grid_spec=pltpu.PrefetchScalarGridSpec(
            num_scalar_prefetch=1,
            grid=(rows // MB,),
            in_specs=[
                rows_spec(D),
                rows_spec(D + LANES),
                rows_spec(D),
                rows_spec(D),
                rows_spec(D),
                rows_spec(D),
                rows_spec(D),
                rows_spec(D + LANES),
                blk((D, WIDE), lambda i, *_: (0, 0), 1),
                rows_spec(LANES),
                rows_spec(LANES),
            ],
            out_specs=[rows_spec(D), blk((D, WIDE), lambda i, *_: (0, 0), 1)],
            scratch_shapes=[pltpu.VMEM((D, WIDE), F32), pltpu.VMEM((8, D), F32)],
        ),
        out_shape=[shape((rows, D), F32), shape((D, WIDE), BF)],
        compiler_params=kernel_params(),
        name="attention_backward",
    )(lengths, tokens, cot, resid, q, kv, mixed, nm, d_mid, packed, cosine, sine)


def rope_tables(lengths):
    ends = jnp.stack([jnp.sum(lengths[:, : s + 1], axis=1) for s in range(lengths.shape[1] - 1)], axis=1)
    index = jnp.arange(MB, dtype=jnp.int32)
    start = jnp.max(jnp.where(ends[:, None, :] <= index[None, :, None], ends[:, None, :], 0), axis=2)
    position = (index[None, :] - start).astype(F32).reshape(-1)
    lane = jnp.arange(LANES, dtype=jnp.int32)
    freq = jnp.exp(-((2 * (lane % (HD // 2))).astype(F32) / HD) * jnp.log(10000.0))
    angle = position[:, None] * freq[None, :]
    sign = jnp.where(lane % HD < HD // 2, -1.0, 1.0)
    return jnp.cos(angle), jnp.sin(angle) * sign[None, :]


def gather(v, axes):
    return lax.all_gather(v, axes, axis=0, tiled=True)


def scatter_sum(v, axes, dim=0):
    return lax.psum_scatter(v, axes, scatter_dimension=dim, tiled=True)


def shards(tokens, cotangent, lengths, routes, attn_gain, w_query, w_keyval, w_out, moe_gain, w_router, w_gateup, w_down):
    rows, share = tokens.shape[0], w_query.shape[0]
    outer = lax.axis_size("z")
    me = lax.axis_index(PLANE_AXES).astype(jnp.int32).reshape(1)

    small = jnp.concatenate(
        [w_router, attn_gain[:, None], moe_gain[:, None], jnp.zeros((share, LANES - E - 2), BF)], axis=1
    )
    packed = gather(jnp.concatenate([w_query, w_keyval, w_out, small], axis=1), ALL)

    sent = jnp.concatenate([w_gateup, w_down], axis=1)
    own = lax.all_to_all(sent.reshape(PLANE, OWN, *sent.shape[1:]), PLANE_AXES, split_axis=0, concat_axis=0, tiled=True)
    homes = []
    for e in range(OWN):
        home = jnp.concatenate(
            [own[:, e, :share].reshape(PLANE * share, D), own[:, e, share:].reshape(PLANE * share // 2, D)], axis=0
        )
        homes.append(gather(home, "z").reshape(outer, -1, D))

    hot = jnp.sum((routes[:, :, None] == jnp.arange(LANES, dtype=jnp.int32)[None, None, :]).astype(F32), axis=1)
    cot = jnp.concatenate([cotangent, hot.astype(BF)], axis=1)
    cot_all = gather(cot, PLANE_AXES)

    cosine, sine = rope_tables(lengths)
    nm, q, kv, mixed, resid = attention_forward(tokens, lengths, packed, cosine, sine)
    nm_all = gather(nm, PLANE_AXES)
    out_part, d_mid_part, expert_grads = experts(me, nm_all, cot_all, packed, homes)
    d_mid = scatter_sum(d_mid_part, PLANE_AXES)
    out_sum = scatter_sum(out_part, PLANE_AXES)
    output = (resid + out_sum.astype(F32)).astype(BF)
    grad_tokens, grads = attention_backward(tokens, lengths, cot, resid, q, kv, mixed, nm, d_mid, packed, cosine, sine)
    grads = scatter_sum(grads.reshape(outer, PLANE * share, WIDE), PLANE_AXES, 1)
    grads = scatter_sum(grads.reshape(outer * share, WIDE), "z").astype(F32)

    back = []
    for e in range(OWN):
        summed = scatter_sum(expert_grads[e].reshape(-1, D), "z")
        back.append(
            jnp.concatenate(
                [
                    summed[: PLANE * share].reshape(PLANE, share, D),
                    summed[PLANE * share :].reshape(PLANE, share // 2, D),
                ],
                axis=1,
            )
        )
    back = lax.all_to_all(jnp.stack(back, axis=1), PLANE_AXES, split_axis=0, concat_axis=0, tiled=True)
    back = back.reshape(E, -1, D).astype(F32)
    return (
        output,
        grad_tokens,
        grads[:, 3 * D + E],
        grads[:, :D],
        grads[:, D : 2 * D],
        grads[:, 2 * D : 3 * D],
        grads[:, 3 * D + E + 1],
        grads[:, 3 * D : 3 * D + E],
        back[:, :share],
        back[:, share:],
    )


def solution(mesh):
    count = mesh.shape["fsdp"]
    inner = Mesh(mesh.devices.reshape(count // PLANE, 2, 2, 2), ALL)
    row, vec, mid = P(ALL, None), P(ALL), P(None, ALL, None)
    return jax.shard_map(
        shards,
        mesh=inner,
        in_specs=(row, row, row, row, vec, row, row, row, vec, row, mid, mid),
        out_specs=(row, row, vec, row, row, row, vec, row, mid, mid),
        check_vma=False,
    )
```

```python
import functools

import jax
import jax.numpy as jnp
from jax import lax
from jax.experimental import pallas as pl
from jax.experimental.pallas import tpu as pltpu
from jax.sharding import Mesh, PartitionSpec as P

D = 1024
HD = 64
FF = 512
E = 16
MB = 256
GROUPS = 8
PLANE = 8
OWN = E // PLANE
LANES = 128
WIDE = 3 * D + LANES
DMID = D + LANES
EPS = 1e-05
NEG = -1e30

BF = jnp.bfloat16
F32 = jnp.float32
PLANE_AXES = ("y", "x", "c")
ALL = ("z", "y", "x", "c")


def dot(a, b, ca=1, cb=0):
    return lax.dot_general(a, b, (((ca,), (cb,)), ((), ())), preferred_element_type=F32)


def mean_rows(v):
    return jnp.sum(v, axis=-1, keepdims=True) * (1.0 / v.shape[-1])


def lane_of(rows):
    return lax.broadcasted_iota(jnp.int32, (rows, LANES), 1)


def turned(t, low):
    return jnp.where(low, pltpu.roll(t, LANES - HD // 2, 1), pltpu.roll(t, HD // 2, 1))


def swap(t):
    return pltpu.roll(t, HD, 1)


def gain_rows(w_ref):
    cols = w_ref[:, 3 * D :].astype(F32).T
    return cols[E : E + 1, :], cols[E + 1 : E + 2, :]


def bias_of(lens_ref, micro):
    row = lax.broadcasted_iota(jnp.int32, (MB, MB), 0)
    col = lax.broadcasted_iota(jnp.int32, (MB, MB), 1)
    start = jnp.zeros((MB, MB), jnp.int32)
    end = jnp.int32(0)
    for s in range(3):
        end = end + lens_ref[micro, s]
        start = jnp.where(row >= end, end, start)
    return jnp.where((col >= start) & (col <= row), 0.0, NEG)


def split_pair(block, half):
    low = lane_of(block.shape[0]) < HD
    other = swap(block)
    here, there = (block, other) if half == 0 else (other, block)
    return jnp.concatenate(
        [jnp.where(low, here, 0.0), jnp.where(low, 0.0, there)], axis=0
    ).astype(BF)


def softmax_pair(score, bias):
    halves = []
    for h in range(2):
        s = score[:, h * MB : (h + 1) * MB] * 0.125 + bias
        e = jnp.exp(s - jnp.max(s, axis=1, keepdims=True))
        halves.append(e * (1.0 / jnp.sum(e, axis=1, keepdims=True)))
    return jnp.concatenate(halves, axis=1)


def attention_forward_kernel(
    micro, outer, place_ref, lens_ref, tok_ref, cot_ref, w_ref, cos_ref, sin_ref,
    nm_ref, q_ref, kv_ref, mixed_ref, resid_ref, weight_ref, *ordering,
):
    if not micro:
        ordered_ref, w_all, sems, out_sem = ordering
        share = D // outer // PLANE
        copies = []
        for p in range(PLANE):
            for s in range(outer):
                z = lax.rem(place_ref[1] + outer - s, outer)
                at = pl.ds(pl.multiple_of((z * PLANE + p) * share, share), share)
                block = w_ref.at[(p * outer + s) * share : (p * outer + s + 1) * share]
                copies.append(pltpu.make_async_copy(block, w_all.at[at], sems.at[p * outer + s]))
        for copy in copies:
            copy.start()
        for copy in copies:
            copy.wait()
        write = pltpu.make_async_copy(w_all, ordered_ref, out_sem)
        write.start()
        w_ref = w_all
    gain_in, gain_mid = gain_rows(w_ref)
    x = tok_ref[...].astype(F32)
    normed = (x * lax.rsqrt(mean_rows(x * x) + EPS) * gain_in).astype(BF)
    q_lin = dot(normed, w_ref[:, :D])
    kv_lin = dot(normed, w_ref[:, D : 2 * D])
    cosine, sine = cos_ref[...], sin_ref[...]
    low = (lane_of(MB) % HD) < HD // 2
    bias = bias_of(lens_ref, micro)
    mixed = []
    for pair in range(GROUPS // 2):
        lanes = slice(pair * LANES, (pair + 1) * LANES)
        k_pair = kv_lin[:, lanes]
        k_pair = k_pair * cosine + turned(k_pair, low) * sine
        v_pair = kv_lin[:, D // 2 + pair * LANES : D // 2 + (pair + 1) * LANES]
        kv_ref[:, lanes] = k_pair.astype(BF)
        kv_ref[:, D // 2 + pair * LANES : D // 2 + (pair + 1) * LANES] = v_pair.astype(BF)
        for half in range(2):
            group = 2 * pair + half
            q = q_lin[:, group * LANES : (group + 1) * LANES]
            q = (q * cosine + turned(q, low) * sine).astype(BF)
            q_ref[:, group * LANES : (group + 1) * LANES] = q
            score = dot(q, split_pair(k_pair, half), 1, 1)
            weight = softmax_pair(score, bias).astype(BF)
            weight_ref[:, group * 2 * MB : (group + 1) * 2 * MB] = weight
            mixed.append(dot(weight, split_pair(v_pair, half)).astype(BF))
    mixed = jnp.concatenate(mixed, axis=1)
    mixed_ref[...] = mixed
    resid = x + dot(mixed, w_ref[:, 2 * D : 3 * D])
    resid_ref[...] = resid
    nm_ref[:, -D:] = (resid * lax.rsqrt(mean_rows(resid * resid) + EPS) * gain_mid).astype(BF)
    if micro:
        nm_ref[:, :DMID] = cot_ref[...]
    else:
        write.wait()


def masked_gates(logits, routed):
    top = jnp.max(jnp.where(routed, logits, NEG), axis=1, keepdims=True)
    e = jnp.where(routed, jnp.exp(jnp.minimum(logits - top, 0.0)), 0.0)
    return e * (1.0 / jnp.sum(e, axis=1, keepdims=True))


def plane_back(place_ref, s, outer, rows):
    z = lax.rem(place_ref[1] + outer - s, outer)
    return pl.ds(pl.multiple_of(z * rows, rows), rows)


def expert_kernel(outer, micro, e, *refs):
    refs = list(refs)
    take = lambda k: [refs.pop(0) for _ in range(k)]
    place_ref, *peers = take(3 if micro else 5)
    wr_ref = take(1)[0]
    homes = take(outer)
    partial_ref = take(1)[0] if e else None
    carried = take(2) if micro else []
    out_ref = take(1)[0]
    dmid_refs = take(2) if micro and e else []
    grads = take(outer) if micro else []
    acc_gu, acc_dn, w_gu, w_dn, sems = take(5)
    old_gu, old_dn = take(2) if micro else (None, None)
    step = pl.program_id(0)
    up_rows, down_rows = D // outer, FF // outer

    def old_copies():
        return [
            pltpu.make_async_copy(source, target, sems.at[outer, k])
            for k, (source, target) in enumerate(zip(carried, (old_gu, old_dn)))
        ]

    @pl.when(step == 0)
    def _():
        copies = []
        for s in range(outer):
            copies += [
                pltpu.make_async_copy(
                    homes[s].at[:up_rows], w_gu.at[plane_back(place_ref, s, outer, up_rows)], sems.at[s, 0]
                ),
                pltpu.make_async_copy(
                    homes[s].at[up_rows:], w_dn.at[plane_back(place_ref, s, outer, down_rows)], sems.at[s, 1]
                ),
            ]
        for copy in copies + (old_copies() if micro else []):
            copy.start()
        acc_gu[...] = jnp.zeros_like(acc_gu)
        acc_dn[...] = jnp.zeros_like(acc_dn)
        for copy in copies:
            copy.wait()

    cots, nms = (peers, peers) if micro else (peers[:2], peers[2:])
    nm = jnp.concatenate([ref[:, -D:] for ref in nms], axis=0)
    cot = jnp.concatenate([ref[:, :D] for ref in cots], axis=0)
    hot = jnp.concatenate([ref[:, D:DMID] for ref in cots], axis=0).astype(F32)
    lane = lane_of(nm.shape[0])
    gates = masked_gates(dot(nm, wr_ref[...]), hot > 0.5)
    expert = place_ref[0] * OWN + e
    combine = jnp.sum(jnp.where(lane == expert, gates, 0.0), axis=1, keepdims=True)
    gateup = dot(nm, w_gu[...])
    gate, up = gateup[:, :FF], gateup[:, FF:]
    s = 1.0 / (1.0 + jnp.exp(-gate))
    silu = gate * s
    act = silu * up
    d_plain = dot(cot, w_dn[...], 1, 1)
    d_combine = jnp.sum(act * d_plain, axis=1, keepdims=True)
    act = (act * combine).astype(BF)
    out = dot(act, w_dn[...])
    d_act = d_plain * combine
    d_gateup = jnp.concatenate(
        [(d_act * up * (s * (1.0 + gate * (1.0 - s)))).astype(BF), (d_act * silu).astype(BF)], axis=1
    )
    d_mid = dot(d_gateup, w_gu[...], 1, 1)
    acc_gu[...] += dot(nm, d_gateup, 0, 0)
    acc_dn[...] += dot(act, cot, 0, 0)
    high = d_combine.astype(BF).astype(F32)
    extra = jnp.where(lane == expert, high, 0.0) + jnp.where(lane == expert + E, d_combine - high, 0.0)
    if e:
        d_mid = d_mid + partial_ref[:, :D].astype(F32)
        extra = extra + partial_ref[:, D:DMID].astype(F32)
        out = out + partial_ref[:, DMID:].astype(F32)
    d_mid = jnp.concatenate([d_mid.astype(BF), extra.astype(BF)], axis=1)
    out = out.astype(BF)
    if not e:
        out_ref[:, :DMID] = d_mid
        out_ref[:, DMID:] = out
    else:
        core = lax.rem(place_ref[0], 2)
        for half in range(2):
            part = slice(half * MB, (half + 1) * MB)
            at = pl.ds(pl.multiple_of((core if half == 0 else 1 - core) * MB, MB), MB)
            if micro:
                out_ref[at, :] = out[part]
                dmid_refs[half][...] = d_mid[part]
            else:
                out_ref[at, :DMID] = d_mid[part]
                out_ref[at, DMID:] = out[part]

    if micro:

        @pl.when(step == pl.num_programs(0) - 1)
        def _():
            for copy in old_copies():
                copy.wait()
            for s in range(outer):
                at = plane_back(place_ref, s, outer, up_rows)
                grads[s][:up_rows] = (acc_gu[at] + old_gu[at]).astype(BF)
                at = plane_back(place_ref, s, outer, down_rows)
                grads[s][up_rows:] = (acc_dn[at] + old_dn[at]).astype(BF)


def join_pair(a0, b0, a1, b1, low):
    return jnp.where(low, a0, b1) + swap(jnp.where(low, a1, b0))


def attention_backward_kernel(last, *refs):
    refs = list(refs)
    take = lambda k: [refs.pop(0) for _ in range(k)]
    (tok_ref, cot_ref, nm_ref, q_ref, kv_ref, mixed_ref, resid_ref, weight_ref, dmid_ref, w_ref, cos_ref, sin_ref) = take(12)
    old = take(8) if last else []
    rows_ref = take(1)[0]
    kept = refs

    gain_in, gain_mid = gain_rows(w_ref)
    lane = lane_of(MB)
    cot = cot_ref[:, :D].astype(F32)
    resid = resid_ref[...]
    nm = nm_ref[:, -D:]
    w_small = w_ref[:, 3 * D :]
    gates = masked_gates(dot(nm, w_small), cot_ref[:, D:].astype(F32) > 0.5)
    pieces = dmid_ref[:, D:].astype(F32)
    d_gates = pieces + pltpu.roll(pieces, LANES - E, 1)
    d_logits = gates * (d_gates - jnp.sum(gates * d_gates, axis=1, keepdims=True))
    d_logits = jnp.where(lane < E, d_logits, 0.0).astype(BF)
    d_mid = dmid_ref[:, :D].astype(F32) + dot(d_logits, w_small, 1, 1)
    inverse = lax.rsqrt(mean_rows(resid * resid) + EPS)
    u = d_mid * gain_mid
    d_resid = cot + inverse * u - resid * (inverse * inverse * inverse) * mean_rows(u * resid)
    gain_mid_grad = jnp.sum(d_mid * resid * inverse, axis=0, keepdims=True)
    d_branch = d_resid.astype(BF)
    d_mixed = dot(d_branch, w_ref[:, 2 * D : 3 * D], 1, 1).astype(BF)

    cosine, sine = cos_ref[...], sin_ref[...]
    low = (lane % HD) < HD // 2
    head_low = lane < HD
    d_q, d_k, d_v = [], [], []
    for pair in range(GROUPS // 2):
        k_pair = kv_ref[:, pair * LANES : (pair + 1) * LANES].astype(F32)
        v_pair = kv_ref[:, D // 2 + pair * LANES : D // 2 + (pair + 1) * LANES].astype(F32)
        keys, values = [], []
        for half in range(2):
            group = 2 * pair + half
            q = q_ref[:, group * LANES : (group + 1) * LANES]
            dm = d_mixed[:, group * LANES : (group + 1) * LANES]
            k_two = split_pair(k_pair, half)
            weight = weight_ref[:, group * 2 * MB : (group + 1) * 2 * MB]
            p = weight.astype(F32)
            d_weight = dot(dm, split_pair(v_pair, half), 1, 1)
            scored = p * d_weight
            d_score = []
            for h in range(2):
                part = slice(h * MB, (h + 1) * MB)
                total = jnp.sum(scored[:, part], axis=1, keepdims=True)
                d_score.append((p[:, part] * (d_weight[:, part] - total)).astype(BF))
            d_score = jnp.concatenate(d_score, axis=1)
            d_query = dot(d_score, k_two) * 0.125
            d_q.append((d_query * cosine - turned(d_query, low) * sine).astype(BF))
            d_key = dot(d_score, q, 0, 0) * 0.125
            d_value = dot(weight, dm, 0, 0)
            keys += [d_key[:MB], d_key[MB:]]
            values += [d_value[:MB], d_value[MB:]]
        d_key = join_pair(*keys, head_low)
        d_k.append((d_key * cosine - turned(d_key, low) * sine).astype(BF))
        d_v.append(join_pair(*values, head_low).astype(BF))
    d_q = jnp.concatenate(d_q, axis=1)
    d_kv = jnp.concatenate(d_k + d_v, axis=1)

    x = tok_ref[...].astype(F32)
    inverse = lax.rsqrt(mean_rows(x * x) + EPS)
    normed = (x * inverse * gain_in).astype(BF)
    d_in = dot(d_q, w_ref[:, :D], 1, 1) + dot(d_kv, w_ref[:, D : 2 * D], 1, 1)
    v = d_in * gain_in
    rows_ref[...] = d_resid + inverse * v - x * (inverse * inverse * inverse) * mean_rows(v * x)
    gain_in_grad = jnp.sum(d_in * x * inverse, axis=0, keepdims=True)
    gains = jnp.concatenate([gain_in_grad, gain_mid_grad, jnp.zeros((6, D), F32)], axis=0)

    if not last:
        for ref, value in zip(kept, (normed, d_q, d_kv, d_branch, d_logits, gains)):
            ref[...] = value
        return
    grad_ref = kept[0]
    both = lambda k, value: jnp.concatenate([old[k][...], value], axis=0)
    normed_two = both(0, normed)
    grad_ref[:, :D] = dot(normed_two, both(1, d_q), 0, 0).astype(BF)
    grad_ref[:, D : 2 * D] = dot(normed_two, both(2, d_kv), 0, 0).astype(BF)
    grad_ref[:, 2 * D : 3 * D] = dot(both(6, mixed_ref[...]), both(3, d_branch), 0, 0).astype(BF)
    gains = jnp.concatenate([jnp.zeros((E, D), F32), gains + old[5][...], jnp.zeros((LANES - E - 8, D), F32)], axis=0)
    grad_ref[:, 3 * D :] = (dot(both(7, nm), both(4, d_logits), 0, 0) + gains.T).astype(BF)


def blk(shape, index, buffers=None):
    if buffers is None:
        return pl.BlockSpec(shape, index)
    return pl.BlockSpec(shape, index, pipeline_mode=pl.Buffered(buffers))


def kernel_params(mib=58):
    return pltpu.CompilerParams(dimension_semantics=("arbitrary",), vmem_limit_bytes=mib << 20)


def takes(us):
    return pl.CostEstimate(flops=int(us * 1.15e9), bytes_accessed=1 << 20, transcendentals=0)


def shaped(rows, width, kind=BF):
    return jax.ShapeDtypeStruct((rows, width), kind)


def own_rows(width, micro=0):
    return blk((MB, width), lambda i, *_: (micro, 0))


def whole(shape):
    return blk(shape, lambda i, *_: (0,) * len(shape), 1)


def attention_forward(micro, outer, place, lengths, tokens, cot, packed, cosine, sine):
    width = DMID + D if micro else D
    any_ref = pl.BlockSpec(memory_space=pl.ANY)
    return pl.pallas_call(
        functools.partial(attention_forward_kernel, micro, outer),
        grid_spec=pltpu.PrefetchScalarGridSpec(
            num_scalar_prefetch=2,
            grid=(1,),
            in_specs=[own_rows(D, micro), own_rows(DMID, micro), whole((D, WIDE)) if micro else any_ref]
            + [own_rows(LANES, micro)] * 2,
            out_specs=[own_rows(width)] + [own_rows(D)] * 4 + [own_rows(D * 4)] + ([] if micro else [any_ref]),
            scratch_shapes=[]
            if micro
            else [pltpu.VMEM((D, WIDE), BF), pltpu.SemaphoreType.DMA((PLANE * outer,)), pltpu.SemaphoreType.DMA],
        ),
        out_shape=[shaped(MB, width)]
        + [shaped(MB, D)] * 3
        + [shaped(MB, D, F32), shaped(MB, D * 4)]
        + ([] if micro else [shaped(D, WIDE)]),
        compiler_params=kernel_params(),
        cost_estimate=takes(12),
        name=f"attention_forward_{micro}",
    )(place, lengths, tokens, cot, packed, cosine, sine)


def experts(micro, e, place, rows, packed, homes, carried=(), partial=()):
    outer = len(homes)
    wide = DMID + D
    any_ref = pl.BlockSpec(memory_space=pl.ANY)
    shape = jax.ShapeDtypeStruct

    def peer(k, width):
        return blk((MB, width), lambda i, place, *_: (lax.bitwise_xor(place[0], 2 * i + k), 0))

    near = blk((MB, DMID), lambda i, *_: (i, 0))
    pair = blk((2 * MB, wide), lambda i, *_: (i, 0))
    home = shape(homes[0].shape, BF)
    acc = [shape((D, 2 * FF), F32), shape((FF, D), F32)]
    in_specs = [peer(0, wide), peer(1, wide)] if micro else [near, near, peer(0, D), peer(1, D)]
    in_specs += [blk((D, LANES), lambda i, *_: (0, 3 * D // LANES), 1)]
    in_specs += [any_ref] * outer + [pair] * len(partial) + [any_ref] * len(carried)
    scratch = [
        pltpu.VMEM((D, 2 * FF), BF),
        pltpu.VMEM((FF, D), BF),
        pltpu.SemaphoreType.DMA((outer + 1, 2)),
    ]
    if not e:
        out_specs, out_shape = [pair], [shaped(PLANE * MB, wide)]
    else:
        width = D if micro else wide
        out_specs = [blk((2 * MB, width), lambda i, place, *_: (lax.bitwise_xor(place[0] // 2, i), 0))]
        out_shape = [shaped(PLANE * MB, width)]
        if micro:
            out_specs += [near, near]
            out_shape += [shaped(PLANE // 2 * MB, DMID)] * 2
    if micro:
        out_specs += [whole(home.shape)] * outer
        out_shape += [home] * outer
        scratch = [pltpu.VMEM(a.shape, F32) for a in acc] + scratch + [pltpu.VMEM(a.shape, F32) for a in acc]
    else:
        out_specs += [whole(a.shape) for a in acc]
        out_shape += acc
    return pl.pallas_call(
        functools.partial(expert_kernel, outer, micro, e),
        grid_spec=pltpu.PrefetchScalarGridSpec(
            num_scalar_prefetch=1,
            grid=(PLANE // 2,),
            in_specs=in_specs,
            out_specs=out_specs,
            scratch_shapes=scratch,
        ),
        out_shape=out_shape,
        compiler_params=kernel_params(),
        cost_estimate=takes(28),
        name=f"experts_{micro}_{e}",
    )(place, *rows, packed, *homes, *partial, *carried)


def attention_backward(micro, tokens, cot, saved, d_mid, packed, cosine, sine, old):
    last = old is not None
    in_specs = [own_rows(D, micro), own_rows(DMID, micro)] + [own_rows(v.shape[1]) for v in saved]
    in_specs += [own_rows(DMID), whole((D, WIDE)), own_rows(LANES, micro), own_rows(LANES, micro)]
    args = [tokens, cot, *saved, d_mid, packed, cosine, sine]
    kept = [shaped(MB, D)] * 4 + [shaped(MB, LANES), shaped(8, D, F32)]
    if last:
        args += old
        in_specs += [whole(a.shape) for a in old]
        kept = [shaped(D, WIDE)]
    return pl.pallas_call(
        functools.partial(attention_backward_kernel, last),
        grid=(1,),
        in_specs=in_specs,
        out_specs=[own_rows(D)] + [whole(a.shape) for a in kept],
        out_shape=[shaped(MB, D, F32)] + kept,
        compiler_params=kernel_params(),
        cost_estimate=takes(22 if last else 16),
        name=f"attention_backward_{micro}",
    )(*args)


def rope_tables(lengths):
    ends = jnp.stack([jnp.sum(lengths[:, : s + 1], axis=1) for s in range(lengths.shape[1] - 1)], axis=1)
    index = jnp.arange(MB, dtype=jnp.int32)
    start = jnp.max(jnp.where(ends[:, None, :] <= index[None, :, None], ends[:, None, :], 0), axis=2)
    position = (index[None, :] - start).astype(F32).reshape(-1)
    lane = jnp.arange(LANES, dtype=jnp.int32)
    freq = jnp.exp(-((2 * (lane % (HD // 2))).astype(F32) / HD) * jnp.log(10000.0))
    angle = position[:, None] * freq[None, :]
    sign = jnp.where(lane % HD < HD // 2, -1.0, 1.0)
    return jnp.cos(angle), jnp.sin(angle) * sign[None, :]


def gather(v, axes):
    return lax.all_gather(v, axes, axis=0, tiled=True)


def scatter_sum(v, axes, dim=0):
    return lax.psum_scatter(v, axes, scatter_dimension=dim, tiled=True)


def tie(*values):
    return lax.optimization_barrier(values)


def after(v, *others):
    return tie(v, *others)[0]


def across(v, axis):
    return lax.ppermute(v, axis, [(0, 1), (1, 0)])


def onward(v, steps=1):
    count = lax.axis_size("z")
    return lax.ppermute(v, "z", [(i, (i + steps) % count) for i in range(count)])


def plus(a, b):
    return (a.astype(F32) + b.astype(F32)).astype(BF)


def pick(v, index, axis):
    return lax.dynamic_index_in_dim(v, index, axis, keepdims=False)


def sum_weights(g, beside):
    outer = g.shape[0]
    z, y, x, c = (lax.axis_index(axis) for axis in ALL)
    cut = g.shape[-1] // 2 // LANES * LANES
    got, _ = tie(across(pick(g, 1 - c, 3), "c"), beside[0]())
    total = plus(pick(g, c, 3), got)
    first, second = total[..., :cut], total[..., cut:]
    got_x, got_y, _ = tie(across(pick(first, 1 - x, 2), "x"), across(pick(second, 1 - y, 1), "y"), beside[1]())
    first, second = plus(pick(first, x, 2), got_x), plus(pick(second, y, 1), got_y)
    got_y, got_x, _ = tie(across(pick(first, 1 - y, 1), "y"), across(pick(second, 1 - x, 1), "x"), beside[2]())
    total = jnp.concatenate([plus(pick(first, y, 1), got_y), plus(pick(second, x, 1), got_x)], axis=-1)
    terms = [pick(total, z, 0)] + [onward(pick(total, (z + s) % outer, 0), s) for s in range(1, outer)]
    return sum(term.astype(F32) for term in terms)


def sum_to_owners(same, other, hold):
    total = plus(same, across(other, "c"))
    total = total.reshape(4, 2, MB // 2, -1)
    first = [total[i, 0] for i in range(4)]
    second = [total[i, 1] for i in range(4)]
    got_x = across(jnp.stack([first[1], first[3]]), "x")
    got_y = across(jnp.stack([second[2], second[3]]), "y")
    got_x, got_y, hold = tie(got_x, got_y, hold)
    last_x, last_y = across(plus(second[1], got_y[1]), "x"), across(plus(first[2], got_x[1]), "y")
    return jnp.concatenate(
        [
            (first[0].astype(F32) + got_x[0].astype(F32) + last_y.astype(F32)).astype(BF),
            (second[0].astype(F32) + got_y[0].astype(F32) + last_x.astype(F32)).astype(BF),
        ],
        axis=0,
    ), hold


def shards(tokens, cotangent, lengths, routes, attn_gain, w_query, w_keyval, w_out, moe_gain, w_router, w_gateup, w_down):
    share = w_query.shape[0]
    outer = lax.axis_size("z")
    place = jnp.stack([lax.axis_index(PLANE_AXES), lax.axis_index("z")]).astype(jnp.int32)

    small = jnp.concatenate(
        [w_router, attn_gain[:, None], moe_gain[:, None], jnp.zeros((share, LANES - E - 2), BF)], axis=1
    )
    own = jnp.concatenate([w_query, w_keyval, w_out, small], axis=1)
    pieces = [own] + [onward(own, s) for s in range(1, outer)]
    sent = jnp.concatenate([w_gateup, w_down], axis=1)
    sent = sent.reshape(PLANE, OWN, *sent.shape[1:])

    def bring(part):
        got = lax.all_to_all(part, PLANE_AXES, split_axis=0, concat_axis=0, tiled=True)
        return jnp.concatenate(
            [got[:, :share].reshape(PLANE * share, D), got[:, share:].reshape(PLANE * share // 2, D)], axis=0
        )

    def ring(e, count=1):
        for _ in range(count):
            homes[e].append(onward(homes[e][-1]))
        return homes[e][-1]

    homes = [[bring(sent[:, 0])], []]
    *pieces, homes[0][0] = tie(*pieces, homes[0][0])
    packed = gather(jnp.concatenate(pieces, axis=0), PLANE_AXES)
    part, homes[0][-1] = tie(sent[:, 1], ring(0))
    homes[1].append(bring(part))
    hot = jnp.sum((routes[:, :, None] == jnp.arange(LANES, dtype=jnp.int32)[None, None, :]).astype(F32), axis=1)
    cot = jnp.concatenate([cotangent, hot.astype(BF)], axis=1)
    cot_0, homes[1][0] = tie(cot[:MB], homes[1][0])
    cosine, sine = rope_tables(lengths)

    from_x, from_y = across(cot_0, "x"), across(cot_0, "y")
    packed, from_x, from_y, homes[0][-1] = tie(packed, from_x, from_y, ring(0, outer - 2))
    *saved_0, packed = attention_forward(0, outer, place, lengths, tokens, cot, packed, cosine, sine)
    nm_0 = gather(saved_0[0], PLANE_AXES)
    corner_a, corner_b = across(from_x[: MB // 2], "y"), across(from_y[MB // 2 :], "x")
    packed, corner_a, corner_b, homes[1][-1] = tie(packed, corner_a, corner_b, ring(1, max(outer - 3, 0)))
    cot_same = jnp.concatenate([cot_0, from_x, from_y, corner_a, corner_b], axis=0)
    saved_1 = attention_forward(1, outer, place, lengths, tokens, cot, packed, cosine, sine)
    nm_1, homes[1][-1] = tie(saved_1[0], ring(1))
    nm_1 = gather(nm_1, PLANE_AXES)
    cot_other = across(cot_same, "c")
    ring(1, outer - len(homes[1]))

    rows = [cot_same, cot_other, nm_0, nm_0]
    partial, *carried_a = experts(0, 0, place, rows, packed, homes[0])
    both_0, *carried_b = experts(0, 1, place, rows, packed, homes[1], partial=[partial])
    rows = [nm_1, nm_1]
    partial, *turns_a = experts(1, 0, place, rows, packed, homes[0], carried_a)
    out_1, same_1, other_1, *turns_b = experts(1, 1, place, rows, packed, homes[1], carried_b, [partial])

    turns = [turns_a, turns_b]
    moved = [turns_a[1], turns_b[1]]

    def pass_on(e, first, last):
        for s in range(first, last):
            moved[e] = onward(moved[e] if s == 1 else plus(turns[e][s], moved[e]))
        return moved[e]

    other_1, moved[0] = tie(other_1, pass_on(0, 1, 2))
    both_0 = scatter_sum(both_0, PLANE_AXES)
    rows_0, *old = attention_backward(0, tokens, cot, saved_0, both_0, packed, cosine, sine, None)
    old = old + [saved_0[3], saved_0[0]]
    d_mid_1, rows_0 = sum_to_owners(same_1, other_1, rows_0)
    d_mid_1, *moved = tie(d_mid_1, pass_on(0, 2, outer - 1), pass_on(1, 1, outer - 2))
    rows_1, grads = attention_backward(1, tokens, cot, saved_1, d_mid_1, packed, cosine, sine, old)
    out_sums = both_0[:, DMID:], scatter_sum(out_1, PLANE_AXES)
    output = [(saved[4] + part.astype(F32)).astype(BF) for saved, part in zip((saved_0, saved_1), out_sums)]
    grads, moved[0] = tie(grads, pass_on(0, outer - 1, outer))

    def send_home(e):
        m = plus(turns[e][0], moved[e])
        m = jnp.concatenate(
            [m[: PLANE * share].reshape(PLANE, share, D), m[PLANE * share :].reshape(PLANE, share // 2, D)], axis=1
        )
        got = lax.all_to_all(m, PLANE_AXES, split_axis=0, concat_axis=0, tiled=True)
        kept.append(got)
        return got

    kept = []
    beside = (
        lambda: send_home(0),
        lambda: pass_on(1, outer - 2, outer - 1),
        lambda: pass_on(1, outer - 1, outer),
    )
    grads = sum_weights(grads.reshape(outer, 2, 2, 2, share, WIDE), beside)
    send_home(1)
    home = jnp.stack(kept, axis=1).reshape(E, -1, D).astype(F32)
    return (
        jnp.concatenate(output, axis=0),
        jnp.concatenate([rows_0, rows_1], axis=0),
        grads[:, 3 * D + E],
        grads[:, :D],
        grads[:, D : 2 * D],
        grads[:, 2 * D : 3 * D],
        grads[:, 3 * D + E + 1],
        grads[:, 3 * D : 3 * D + E],
        home[:, :share],
        home[:, share:],
    )


def solution(mesh):
    count = mesh.shape["fsdp"]
    inner = Mesh(mesh.devices.reshape(count // PLANE, 2, 2, 2), ALL)
    row, vec, mid = P(ALL, None), P(ALL), P(None, ALL, None)
    return jax.shard_map(
        shards,
        mesh=inner,
        in_specs=(row, row, row, row, vec, row, row, row, vec, row, mid, mid),
        out_specs=(row, row, vec, row, row, row, vec, row, mid, mid),
        check_vma=False,
    )
```

```python
import functools

import jax
import jax.numpy as jnp
from jax import lax
from jax.experimental import pallas as pl
from jax.experimental.pallas import tpu as pltpu
from jax.sharding import Mesh, PartitionSpec as P

D = 1024
HD = 64
FF = 512
E = 16
MB = 256
GROUPS = 8
PLANE = 8
OWN = E // PLANE
LANES = 128
WIDE = 3 * D + LANES
DMID = D + LANES
EPS = 1e-05
NEG = -1e30

BF = jnp.bfloat16
F32 = jnp.float32
PLANE_AXES = ("y", "x", "c")
ALL = ("z", "y", "x", "c")


def dot(a, b, ca=1, cb=0):
    return lax.dot_general(a, b, (((ca,), (cb,)), ((), ())), preferred_element_type=F32)


def mean_rows(v):
    return jnp.sum(v, axis=-1, keepdims=True) * (1.0 / v.shape[-1])


def lane_of(rows):
    return lax.broadcasted_iota(jnp.int32, (rows, LANES), 1)


def turned(t, low):
    return jnp.where(low, pltpu.roll(t, LANES - HD // 2, 1), pltpu.roll(t, HD // 2, 1))


def swap(t):
    return pltpu.roll(t, HD, 1)


def gain_rows(w_ref):
    cols = w_ref[:, 3 * D :].astype(F32).T
    return cols[E : E + 1, :], cols[E + 1 : E + 2, :]


def bias_of(lens_ref, micro):
    row = lax.broadcasted_iota(jnp.int32, (MB, MB), 0)
    col = lax.broadcasted_iota(jnp.int32, (MB, MB), 1)
    start = jnp.zeros((MB, MB), jnp.int32)
    end = jnp.int32(0)
    for s in range(3):
        end = end + lens_ref[micro, s]
        start = jnp.where(row >= end, end, start)
    return jnp.where((col >= start) & (col <= row), 0.0, NEG)


def split_pair(block, half):
    low = lane_of(block.shape[0]) < HD
    other = swap(block)
    here, there = (block, other) if half == 0 else (other, block)
    return jnp.concatenate(
        [jnp.where(low, here, 0.0), jnp.where(low, 0.0, there)], axis=0
    ).astype(BF)


def softmax_pair(score, bias):
    halves = []
    for h in range(2):
        s = score[:, h * MB : (h + 1) * MB] * 0.125 + bias
        e = jnp.exp(s - jnp.max(s, axis=1, keepdims=True))
        halves.append(e * (1.0 / jnp.sum(e, axis=1, keepdims=True)))
    return jnp.concatenate(halves, axis=1)


def attention_forward_kernel(
    micro, outer, place_ref, lens_ref, tok_ref, cot_ref, w_ref, cos_ref, sin_ref,
    nm_ref, q_ref, kv_ref, mixed_ref, resid_ref, weight_ref, *ordering,
):
    if not micro:
        ordered_ref, w_all, sems, out_sem = ordering
        share = D // outer // PLANE
        copies = []
        for p in range(PLANE):
            for s in range(outer):
                z = lax.rem(place_ref[1] + outer - s, outer)
                at = pl.ds(pl.multiple_of((z * PLANE + p) * share, share), share)
                block = w_ref.at[(p * outer + s) * share : (p * outer + s + 1) * share]
                copies.append(pltpu.make_async_copy(block, w_all.at[at], sems.at[p * outer + s]))
        for copy in copies:
            copy.start()
        for copy in copies:
            copy.wait()
        write = pltpu.make_async_copy(w_all, ordered_ref, out_sem)
        write.start()
        w_ref = w_all
    gain_in, gain_mid = gain_rows(w_ref)
    x = tok_ref[...].astype(F32)
    normed = (x * lax.rsqrt(mean_rows(x * x) + EPS) * gain_in).astype(BF)
    q_lin = dot(normed, w_ref[:, :D])
    kv_lin = dot(normed, w_ref[:, D : 2 * D])
    cosine, sine = cos_ref[...], sin_ref[...]
    low = (lane_of(MB) % HD) < HD // 2
    bias = bias_of(lens_ref, micro)
    mixed = []
    for pair in range(GROUPS // 2):
        lanes = slice(pair * LANES, (pair + 1) * LANES)
        k_pair = kv_lin[:, lanes]
        k_pair = k_pair * cosine + turned(k_pair, low) * sine
        v_pair = kv_lin[:, D // 2 + pair * LANES : D // 2 + (pair + 1) * LANES]
        kv_ref[:, lanes] = k_pair.astype(BF)
        kv_ref[:, D // 2 + pair * LANES : D // 2 + (pair + 1) * LANES] = v_pair.astype(BF)
        for half in range(2):
            group = 2 * pair + half
            q = q_lin[:, group * LANES : (group + 1) * LANES]
            q = (q * cosine + turned(q, low) * sine).astype(BF)
            q_ref[:, group * LANES : (group + 1) * LANES] = q
            score = dot(q, split_pair(k_pair, half), 1, 1)
            weight = softmax_pair(score, bias).astype(BF)
            weight_ref[:, group * 2 * MB : (group + 1) * 2 * MB] = weight
            mixed.append(dot(weight, split_pair(v_pair, half)).astype(BF))
    mixed = jnp.concatenate(mixed, axis=1)
    mixed_ref[...] = mixed
    resid = x + dot(mixed, w_ref[:, 2 * D : 3 * D])
    resid_ref[...] = resid
    nm_ref[:, -D:] = (resid * lax.rsqrt(mean_rows(resid * resid) + EPS) * gain_mid).astype(BF)
    if micro:
        nm_ref[:, :DMID] = cot_ref[...]
    else:
        write.wait()


def masked_gates(logits, routed):
    top = jnp.max(jnp.where(routed, logits, NEG), axis=1, keepdims=True)
    e = jnp.where(routed, jnp.exp(jnp.minimum(logits - top, 0.0)), 0.0)
    return e * (1.0 / jnp.sum(e, axis=1, keepdims=True))


def plane_back(place_ref, s, outer, rows):
    z = lax.rem(place_ref[1] + outer - s, outer)
    return pl.ds(pl.multiple_of(z * rows, rows), rows)


def expert_kernel(outer, micro, e, *refs):
    refs = list(refs)
    take = lambda k: [refs.pop(0) for _ in range(k)]
    place_ref, *peers = take(3 if micro else 5)
    wr_ref = take(1)[0]
    homes = take(outer)
    partial_ref = take(1)[0] if e else None
    carried = take(2) if micro else []
    out_ref = take(1)[0]
    dmid_refs = take(2) if micro and e else []
    grads = take(outer) if micro else []
    acc_gu, acc_dn, w_gu, w_dn, sems = take(5)
    old_gu, old_dn = take(2) if micro else (None, None)
    step = pl.program_id(0)
    up_rows, down_rows = D // outer, FF // outer

    def old_copies():
        return [
            pltpu.make_async_copy(source, target, sems.at[outer, k])
            for k, (source, target) in enumerate(zip(carried, (old_gu, old_dn)))
        ]

    @pl.when(step == 0)
    def _():
        copies = []
        for s in range(outer):
            copies += [
                pltpu.make_async_copy(
                    homes[s].at[:up_rows], w_gu.at[plane_back(place_ref, s, outer, up_rows)], sems.at[s, 0]
                ),
                pltpu.make_async_copy(
                    homes[s].at[up_rows:], w_dn.at[plane_back(place_ref, s, outer, down_rows)], sems.at[s, 1]
                ),
            ]
        for copy in copies + (old_copies() if micro else []):
            copy.start()
        acc_gu[...] = jnp.zeros_like(acc_gu)
        acc_dn[...] = jnp.zeros_like(acc_dn)
        for copy in copies:
            copy.wait()

    cots, nms = (peers, peers) if micro else (peers[:2], peers[2:])
    nm = jnp.concatenate([ref[:, -D:] for ref in nms], axis=0)
    cot = jnp.concatenate([ref[:, :D] for ref in cots], axis=0)
    hot = jnp.concatenate([ref[:, D:DMID] for ref in cots], axis=0).astype(F32)
    lane = lane_of(nm.shape[0])
    gates = masked_gates(dot(nm, wr_ref[...]), hot > 0.5)
    expert = place_ref[0] * OWN + e
    combine = jnp.sum(jnp.where(lane == expert, gates, 0.0), axis=1, keepdims=True)
    gateup = dot(nm, w_gu[...])
    gate, up = gateup[:, :FF], gateup[:, FF:]
    s = 1.0 / (1.0 + jnp.exp(-gate))
    silu = gate * s
    act = silu * up
    d_plain = dot(cot, w_dn[...], 1, 1)
    d_combine = jnp.sum(act * d_plain, axis=1, keepdims=True)
    act = (act * combine).astype(BF)
    out = dot(act, w_dn[...])
    d_act = d_plain * combine
    d_gateup = jnp.concatenate(
        [(d_act * up * (s * (1.0 + gate * (1.0 - s)))).astype(BF), (d_act * silu).astype(BF)], axis=1
    )
    d_mid = dot(d_gateup, w_gu[...], 1, 1)
    acc_gu[...] += dot(nm, d_gateup, 0, 0)
    acc_dn[...] += dot(act, cot, 0, 0)
    high = d_combine.astype(BF).astype(F32)
    extra = jnp.where(lane == expert, high, 0.0) + jnp.where(lane == expert + E, d_combine - high, 0.0)
    if e:
        d_mid = d_mid + partial_ref[:, :D].astype(F32)
        extra = extra + partial_ref[:, D:DMID].astype(F32)
        out = out + partial_ref[:, DMID:].astype(F32)
    d_mid = jnp.concatenate([d_mid.astype(BF), extra.astype(BF)], axis=1)
    out = out.astype(BF)
    if not e:
        out_ref[:, :DMID] = d_mid
        out_ref[:, DMID:] = out
    else:
        core = lax.rem(place_ref[0], 2)
        for half in range(2):
            part = slice(half * MB, (half + 1) * MB)
            at = pl.ds(pl.multiple_of((core if half == 0 else 1 - core) * MB, MB), MB)
            if micro:
                out_ref[at, :] = out[part]
                dmid_refs[half][...] = d_mid[part]
            else:
                out_ref[at, :DMID] = d_mid[part]
                out_ref[at, DMID:] = out[part]

    if micro:

        @pl.when(step == pl.num_programs(0) - 1)
        def _():
            for copy in old_copies():
                copy.wait()
            for s in range(outer):
                at = plane_back(place_ref, s, outer, up_rows)
                grads[s][:up_rows] = (acc_gu[at] + old_gu[at]).astype(BF)
                at = plane_back(place_ref, s, outer, down_rows)
                grads[s][up_rows:] = (acc_dn[at] + old_dn[at]).astype(BF)


def join_pair(a0, b0, a1, b1, low):
    return jnp.where(low, a0, b1) + swap(jnp.where(low, a1, b0))


def attention_backward_kernel(outer, last, *refs):
    refs = list(refs)
    take = lambda k: [refs.pop(0) for _ in range(k)]
    place_ref = take(1)[0]
    (tok_ref, cot_ref, nm_ref, q_ref, kv_ref, mixed_ref, resid_ref, weight_ref, dmid_ref, w_ref, cos_ref, sin_ref) = take(12)
    old = take(8) if last else []
    rows_ref = take(1)[0]
    kept = take(2 if last else 6)
    gain_in, gain_mid = gain_rows(w_ref)
    lane = lane_of(MB)
    cot = cot_ref[:, :D].astype(F32)
    resid = resid_ref[...]
    nm = nm_ref[:, -D:]
    w_small = w_ref[:, 3 * D :]
    gates = masked_gates(dot(nm, w_small), cot_ref[:, D:].astype(F32) > 0.5)
    pieces = dmid_ref[:, D:].astype(F32)
    d_gates = pieces + pltpu.roll(pieces, LANES - E, 1)
    d_logits = gates * (d_gates - jnp.sum(gates * d_gates, axis=1, keepdims=True))
    d_logits = jnp.where(lane < E, d_logits, 0.0).astype(BF)
    d_mid = dmid_ref[:, :D].astype(F32) + dot(d_logits, w_small, 1, 1)
    inverse = lax.rsqrt(mean_rows(resid * resid) + EPS)
    u = d_mid * gain_mid
    d_resid = cot + inverse * u - resid * (inverse * inverse * inverse) * mean_rows(u * resid)
    gain_mid_grad = jnp.sum(d_mid * resid * inverse, axis=0, keepdims=True)
    d_branch = d_resid.astype(BF)
    d_mixed = dot(d_branch, w_ref[:, 2 * D : 3 * D], 1, 1).astype(BF)

    cosine, sine = cos_ref[...], sin_ref[...]
    low = (lane % HD) < HD // 2
    head_low = lane < HD
    d_q, d_k, d_v = [], [], []
    for pair in range(GROUPS // 2):
        k_pair = kv_ref[:, pair * LANES : (pair + 1) * LANES].astype(F32)
        v_pair = kv_ref[:, D // 2 + pair * LANES : D // 2 + (pair + 1) * LANES].astype(F32)
        keys, values = [], []
        for half in range(2):
            group = 2 * pair + half
            q = q_ref[:, group * LANES : (group + 1) * LANES]
            dm = d_mixed[:, group * LANES : (group + 1) * LANES]
            k_two = split_pair(k_pair, half)
            weight = weight_ref[:, group * 2 * MB : (group + 1) * 2 * MB]
            p = weight.astype(F32)
            d_weight = dot(dm, split_pair(v_pair, half), 1, 1)
            scored = p * d_weight
            d_score = []
            for h in range(2):
                part = slice(h * MB, (h + 1) * MB)
                total = jnp.sum(scored[:, part], axis=1, keepdims=True)
                d_score.append((p[:, part] * (d_weight[:, part] - total)).astype(BF))
            d_score = jnp.concatenate(d_score, axis=1)
            d_query = dot(d_score, k_two) * 0.125
            d_q.append((d_query * cosine - turned(d_query, low) * sine).astype(BF))
            d_key = dot(d_score, q, 0, 0) * 0.125
            d_value = dot(weight, dm, 0, 0)
            keys += [d_key[:MB], d_key[MB:]]
            values += [d_value[:MB], d_value[MB:]]
        d_key = join_pair(*keys, head_low)
        d_k.append((d_key * cosine - turned(d_key, low) * sine).astype(BF))
        d_v.append(join_pair(*values, head_low).astype(BF))
    d_q = jnp.concatenate(d_q, axis=1)
    d_kv = jnp.concatenate(d_k + d_v, axis=1)

    x = tok_ref[...].astype(F32)
    inverse = lax.rsqrt(mean_rows(x * x) + EPS)
    normed = (x * inverse * gain_in).astype(BF)
    d_in = dot(d_q, w_ref[:, :D], 1, 1) + dot(d_kv, w_ref[:, D : 2 * D], 1, 1)
    v = d_in * gain_in
    rows_ref[...] = d_resid + inverse * v - x * (inverse * inverse * inverse) * mean_rows(v * x)
    gain_in_grad = jnp.sum(d_in * x * inverse, axis=0, keepdims=True)
    gains = jnp.concatenate([gain_in_grad, gain_mid_grad, jnp.zeros((6, D), F32)], axis=0)
    if not last:
        for ref, value in zip(kept, (normed, d_q, d_kv, d_branch, d_logits, gains)):
            ref[...] = value
        return
    both = lambda k, value: jnp.concatenate([old[k][...], value], axis=0)
    grad_ref, sems = refs
    normed_two = both(0, normed)
    grad_ref[:, :D] = dot(normed_two, both(1, d_q), 0, 0).astype(BF)
    grad_ref[:, D : 2 * D] = dot(normed_two, both(2, d_kv), 0, 0).astype(BF)
    grad_ref[:, 2 * D : 3 * D] = dot(both(6, mixed_ref[...]), both(3, d_branch), 0, 0).astype(BF)
    gains = jnp.concatenate([jnp.zeros((E, D), F32), gains + old[5][...], jnp.zeros((LANES - E - 8, D), F32)], axis=0)
    grad_ref[:, 3 * D :] = (dot(both(7, nm), both(4, d_logits), 0, 0) + gains.T).astype(BF)
    share = D // outer // PLANE
    copies = []
    for s in range(outer):
        z = lax.rem(place_ref[1] + s, outer)
        for q in range(PLANE // 2):
            for other in range(2):
                device = lax.bitwise_xor(place_ref[0], 2 * q + other)
                at = pl.ds(pl.multiple_of((z * PLANE + device) * share, share), share)
                sem = sems.at[s * PLANE + 2 * q + other]
                copies.append(pltpu.make_async_copy(grad_ref.at[at], kept[other].at[s, q], sem))
    for copy in copies:
        copy.start()
    for copy in copies:
        copy.wait()


def blk(shape, index, buffers=None):
    if buffers is None:
        return pl.BlockSpec(shape, index)
    return pl.BlockSpec(shape, index, pipeline_mode=pl.Buffered(buffers))


def kernel_params(mib=58):
    return pltpu.CompilerParams(dimension_semantics=("arbitrary",), vmem_limit_bytes=mib << 20)


def takes(us):
    return pl.CostEstimate(flops=int(us * 1.15e9), bytes_accessed=1 << 20, transcendentals=0)


def shaped(rows, width, kind=BF):
    return jax.ShapeDtypeStruct((rows, width), kind)


def own_rows(width, micro=0):
    return blk((MB, width), lambda i, *_: (micro, 0))


def whole(shape):
    return blk(shape, lambda i, *_: (0,) * len(shape), 1)


def attention_forward(micro, outer, place, lengths, tokens, cot, packed, cosine, sine):
    width = DMID + D if micro else D
    any_ref = pl.BlockSpec(memory_space=pl.ANY)
    return pl.pallas_call(
        functools.partial(attention_forward_kernel, micro, outer),
        grid_spec=pltpu.PrefetchScalarGridSpec(
            num_scalar_prefetch=2,
            grid=(1,),
            in_specs=[own_rows(D, micro), own_rows(DMID, micro), whole((D, WIDE)) if micro else any_ref]
            + [own_rows(LANES, micro)] * 2,
            out_specs=[own_rows(width)] + [own_rows(D)] * 4 + [own_rows(D * 4)] + ([] if micro else [any_ref]),
            scratch_shapes=[]
            if micro
            else [pltpu.VMEM((D, WIDE), BF), pltpu.SemaphoreType.DMA((PLANE * outer,)), pltpu.SemaphoreType.DMA],
        ),
        out_shape=[shaped(MB, width)]
        + [shaped(MB, D)] * 3
        + [shaped(MB, D, F32), shaped(MB, D * 4)]
        + ([] if micro else [shaped(D, WIDE)]),
        compiler_params=kernel_params(),
        cost_estimate=takes(12),
        name=f"attention_forward_{micro}",
    )(place, lengths, tokens, cot, packed, cosine, sine)


def experts(micro, e, place, rows, packed, homes, carried=(), partial=()):
    outer = len(homes)
    wide = DMID + D
    any_ref = pl.BlockSpec(memory_space=pl.ANY)
    shape = jax.ShapeDtypeStruct

    def peer(k, width):
        return blk((MB, width), lambda i, place, *_: (lax.bitwise_xor(place[0], 2 * i + k), 0))

    near = blk((MB, DMID), lambda i, *_: (i, 0))
    pair = blk((2 * MB, wide), lambda i, *_: (i, 0))
    home = shape(homes[0].shape, BF)
    acc = [shape((D, 2 * FF), F32), shape((FF, D), F32)]
    in_specs = [peer(0, wide), peer(1, wide)] if micro else [near, near, peer(0, D), peer(1, D)]
    in_specs += [blk((D, LANES), lambda i, *_: (0, 3 * D // LANES), 1)]
    in_specs += [any_ref] * outer + [pair] * len(partial) + [any_ref] * len(carried)
    scratch = [
        pltpu.VMEM((D, 2 * FF), BF),
        pltpu.VMEM((FF, D), BF),
        pltpu.SemaphoreType.DMA((outer + 1, 2)),
    ]
    if not e:
        out_specs, out_shape = [pair], [shaped(PLANE * MB, wide)]
    else:
        width = D if micro else wide
        out_specs = [blk((2 * MB, width), lambda i, place, *_: (lax.bitwise_xor(place[0] // 2, i), 0))]
        out_shape = [shaped(PLANE * MB, width)]
        if micro:
            out_specs += [near, near]
            out_shape += [shaped(PLANE // 2 * MB, DMID)] * 2
    if micro:
        out_specs += [whole(home.shape)] * outer
        out_shape += [home] * outer
        scratch = [pltpu.VMEM(a.shape, F32) for a in acc] + scratch + [pltpu.VMEM(a.shape, F32) for a in acc]
    else:
        out_specs += [whole(a.shape) for a in acc]
        out_shape += acc
    return pl.pallas_call(
        functools.partial(expert_kernel, outer, micro, e),
        grid_spec=pltpu.PrefetchScalarGridSpec(
            num_scalar_prefetch=1,
            grid=(PLANE // 2,),
            in_specs=in_specs,
            out_specs=out_specs,
            scratch_shapes=scratch,
        ),
        out_shape=out_shape,
        compiler_params=kernel_params(),
        cost_estimate=takes(28),
        name=f"experts_{micro}_{e}",
    )(place, *rows, packed, *homes, *partial, *carried)


def attention_backward(micro, outer, place, tokens, cot, saved, d_mid, packed, cosine, sine, old):
    last = old is not None
    any_ref = pl.BlockSpec(memory_space=pl.ANY)
    in_specs = [own_rows(D, micro), own_rows(DMID, micro)] + [own_rows(v.shape[1]) for v in saved]
    in_specs += [own_rows(DMID), whole((D, WIDE)), own_rows(LANES, micro), own_rows(LANES, micro)]
    args = [tokens, cot, *saved, d_mid, packed, cosine, sine]
    kept = [shaped(MB, D)] * 4 + [shaped(MB, LANES), shaped(8, D, F32)]
    kept_specs = [whole(a.shape) for a in kept]
    scratch = []
    if last:
        args += old
        in_specs += [whole(a.shape) for a in old]
        share = D // outer // PLANE
        kept = [jax.ShapeDtypeStruct((outer, PLANE // 2, share, WIDE), BF)] * 2
        kept_specs = [any_ref] * 2
        scratch = [pltpu.VMEM((D, WIDE), BF), pltpu.SemaphoreType.DMA((outer * PLANE,))]
    return pl.pallas_call(
        functools.partial(attention_backward_kernel, outer, last),
        grid_spec=pltpu.PrefetchScalarGridSpec(
            num_scalar_prefetch=1,
            grid=(1,),
            in_specs=in_specs,
            out_specs=[own_rows(D)] + kept_specs,
            scratch_shapes=scratch,
        ),
        out_shape=[shaped(MB, D, F32)] + kept,
        compiler_params=kernel_params(),
        cost_estimate=takes(18 if last else 13),
        name=f"attention_backward_{micro}",
    )(place, *args)


def rope_tables(lengths):
    ends = jnp.stack([jnp.sum(lengths[:, : s + 1], axis=1) for s in range(lengths.shape[1] - 1)], axis=1)
    index = jnp.arange(MB, dtype=jnp.int32)
    start = jnp.max(jnp.where(ends[:, None, :] <= index[None, :, None], ends[:, None, :], 0), axis=2)
    position = (index[None, :] - start).astype(F32).reshape(-1)
    lane = jnp.arange(LANES, dtype=jnp.int32)
    freq = jnp.exp(-((2 * (lane % (HD // 2))).astype(F32) / HD) * jnp.log(10000.0))
    angle = position[:, None] * freq[None, :]
    sign = jnp.where(lane % HD < HD // 2, -1.0, 1.0)
    return jnp.cos(angle), jnp.sin(angle) * sign[None, :]


def gather(v, axes):
    return lax.all_gather(v, axes, axis=0, tiled=True)


def scatter_sum(v, axes, dim=0):
    return lax.psum_scatter(v, axes, scatter_dimension=dim, tiled=True)


def tie(*values):
    return lax.optimization_barrier(values)


def after(v, *others):
    return tie(v, *others)[0]


def across(v, axis):
    return lax.ppermute(v, axis, [(0, 1), (1, 0)])


def onward(v, steps=1):
    count = lax.axis_size("z")
    return lax.ppermute(v, "z", [(i, (i + steps) % count) for i in range(count)])


def plus(a, b):
    return (a.astype(F32) + b.astype(F32)).astype(BF)


def sum_weights(same, other, beside):
    outer = same.shape[0]
    cut = same.shape[-1] // 2 // LANES * LANES

    def both(stage, *values):
        start, took = beside[stage]
        *values, extra = tie(*values, start())
        took(extra)
        return values

    total = plus(same, across(other, "c"))
    first, second = total[..., :cut], total[..., cut:]
    got_x, got_y = both(0, across(first[:, 1::2], "x"), across(second[:, 2:], "y"))
    first, second = plus(first[:, ::2], got_x), plus(second[:, :2], got_y)
    got_y, got_x = both(1, across(first[:, 1], "y"), across(second[:, 1], "x"))
    total = jnp.concatenate([plus(first[:, 0], got_y), plus(second[:, 0], got_x)], axis=-1)
    terms = [total[0]] + [onward(total[s], s) for s in range(1, outer)]
    return sum(term.astype(F32) for term in terms)


def sum_to_owners(same, other, early, late):
    total = plus(same, across(other, "c"))
    total = total.reshape(4, 2, MB // 2, -1)
    first = [total[i, 0] for i in range(4)]
    second = [total[i, 1] for i in range(4)]
    got_x = across(jnp.stack([first[1], first[3]]), "x")
    got_y = across(jnp.stack([second[2], second[3]]), "y")
    got_x, got_y, early = tie(got_x, got_y, early)
    last_x, last_y = across(plus(second[1], got_y[1]), "x"), across(plus(first[2], got_x[1]), "y")
    last_x, last_y, late = tie(last_x, last_y, late)
    return jnp.concatenate(
        [
            (first[0].astype(F32) + got_x[0].astype(F32) + last_y.astype(F32)).astype(BF),
            (second[0].astype(F32) + got_y[0].astype(F32) + last_x.astype(F32)).astype(BF),
        ],
        axis=0,
    ), early, late


def shards(tokens, cotangent, lengths, routes, attn_gain, w_query, w_keyval, w_out, moe_gain, w_router, w_gateup, w_down):
    share = w_query.shape[0]
    outer = lax.axis_size("z")
    place = jnp.stack([lax.axis_index(PLANE_AXES), lax.axis_index("z")]).astype(jnp.int32)

    small = jnp.concatenate(
        [w_router, attn_gain[:, None], moe_gain[:, None], jnp.zeros((share, LANES - E - 2), BF)], axis=1
    )
    own = jnp.concatenate([w_query, w_keyval, w_out, small], axis=1)
    pieces = [own] + [onward(own, s) for s in range(1, outer)]
    sent = jnp.concatenate([w_gateup, w_down], axis=1)
    got = lax.all_to_all(
        sent.reshape(PLANE, OWN, *sent.shape[1:]), PLANE_AXES, split_axis=0, concat_axis=0, tiled=True
    )
    homes = [
        [jnp.concatenate([got[:, e, :share].reshape(-1, D), got[:, e, share:].reshape(-1, D)], axis=0)]
        for e in range(OWN)
    ]
    *pieces, homes[0][0], homes[1][0] = tie(*pieces, homes[0][0], homes[1][0])
    packed = gather(jnp.concatenate(pieces, axis=0), PLANE_AXES)

    def ring(e, count=1):
        for _ in range(count):
            homes[e].append(onward(homes[e][-1]))
        return homes[e][-1]

    hot = jnp.sum((routes[:, :, None] == jnp.arange(LANES, dtype=jnp.int32)[None, None, :]).astype(F32), axis=1)
    cot = jnp.concatenate([cotangent, hot.astype(BF)], axis=1)
    cosine, sine = rope_tables(lengths)

    packed, homes[0][-1] = tie(packed, ring(0, outer - 2))
    cot_0 = after(cot[:MB], homes[0][-1])
    from_x, from_y = across(cot_0, "x"), across(cot_0, "y")
    *saved_0, packed = attention_forward(0, outer, place, lengths, tokens, cot, packed, cosine, sine)
    nm_0, from_x, from_y, homes[0][-1] = tie(saved_0[0], from_x, from_y, ring(0))
    nm_0 = gather(nm_0, PLANE_AXES)
    packed, homes[1][-1] = tie(packed, ring(1, max(outer - 3, 0)))
    corner_a, corner_b = across(from_x[: MB // 2], "y"), across(from_y[MB // 2 :], "x")
    saved_1 = attention_forward(1, outer, place, lengths, tokens, cot, packed, cosine, sine)
    nm_1, corner_a, corner_b, homes[1][-1] = tie(saved_1[0], corner_a, corner_b, ring(1))
    cot_same = jnp.concatenate([cot_0, from_x, from_y, corner_a, corner_b], axis=0)
    nm_1 = gather(nm_1, PLANE_AXES)
    cot_other = across(cot_same, "c")
    ring(1, outer - len(homes[1]))

    rows = [cot_same, cot_other, nm_0, nm_0]
    partial, *carried_a = experts(0, 0, place, rows, packed, homes[0])
    both_0, *carried_b = experts(0, 1, place, rows, packed, homes[1], partial=[partial])
    rows = [nm_1, nm_1]
    partial, *turns_a = experts(1, 0, place, rows, packed, homes[0], carried_a)
    out_1, same_1, other_1, *turns_b = experts(1, 1, place, rows, packed, homes[1], carried_b, [partial])

    turns = [turns_a, turns_b]
    moved = [turns_a[1], turns_b[1]]

    def pass_on(e, first, last):
        for s in range(first, last):
            moved[e] = onward(moved[e] if s == 1 else plus(turns[e][s], moved[e]))
        return moved[e]

    other_1, moved[0] = tie(other_1, pass_on(0, 1, 2))
    both_0 = scatter_sum(both_0, PLANE_AXES)
    rows_0, *old = attention_backward(0, outer, place, tokens, cot, saved_0, both_0, packed, cosine, sine, None)
    old = old + [saved_0[3], saved_0[0]]
    early = rows_0, pass_on(0, 2, outer - 1)
    moved[1] = after(moved[1], rows_0)
    d_mid_1, (rows_0, moved[0]), moved[1] = sum_to_owners(same_1, other_1, early, pass_on(1, 1, outer - 2))
    rows_1, grads, grads_other = attention_backward(1, outer, place, tokens, cot, saved_1, d_mid_1, packed, cosine, sine, old)
    out_sums = both_0[:, DMID:], scatter_sum(out_1, PLANE_AXES)
    output = [(saved[4] + part.astype(F32)).astype(BF) for saved, part in zip((saved_0, saved_1), out_sums)]
    grads, grads_other, moved[0], output[1] = tie(grads, grads_other, pass_on(0, outer - 1, outer), output[1])

    beside = (
        (lambda: pass_on(1, outer - 2, outer - 1), lambda v: moved.__setitem__(1, v)),
        (lambda: pass_on(1, outer - 1, outer), lambda v: moved.__setitem__(1, v)),
    )
    grads = sum_weights(grads, grads_other, beside)
    home = jnp.stack([plus(turns[e][0], moved[e]) for e in range(OWN)])
    up, down = home[:, : PLANE * share], home[:, PLANE * share :]
    home = jnp.concatenate(
        [up.reshape(OWN, PLANE, share, D), down.reshape(OWN, PLANE, share // 2, D)], axis=2
    ).transpose(1, 0, 2, 3)
    home = lax.all_to_all(home, PLANE_AXES, split_axis=0, concat_axis=0, tiled=True)
    home = home.reshape(E, -1, D).astype(F32)
    return (
        jnp.concatenate(output, axis=0),
        jnp.concatenate([rows_0, rows_1], axis=0),
        grads[:, 3 * D + E],
        grads[:, :D],
        grads[:, D : 2 * D],
        grads[:, 2 * D : 3 * D],
        grads[:, 3 * D + E + 1],
        grads[:, 3 * D : 3 * D + E],
        home[:, :share],
        home[:, share:],
    )


def solution(mesh):
    count = mesh.shape["fsdp"]
    inner = Mesh(mesh.devices.reshape(count // PLANE, 2, 2, 2), ALL)
    row, vec, mid = P(ALL, None), P(ALL), P(None, ALL, None)
    return jax.shard_map(
        shards,
        mesh=inner,
        in_specs=(row, row, row, row, vec, row, row, row, vec, row, mid, mid),
        out_specs=(row, row, vec, row, row, row, vec, row, mid, mid),
        check_vma=False,
    )
```

```python
import functools

import jax
import jax.numpy as jnp
from jax import lax
from jax.experimental import pallas as pl
from jax.experimental.pallas import tpu as pltpu
from jax.sharding import Mesh, PartitionSpec as P

D = 1024
HD = 64
FF = 512
E = 16
MB = 256
GROUPS = 8
PLANE = 8
OWN = E // PLANE
LANES = 128
WIDE = 3 * D + LANES
DMID = D + LANES
EPS = 1e-05
NEG = -1e30

BF = jnp.bfloat16
F32 = jnp.float32
PLANE_AXES = ("y", "x", "c")
ALL = ("z", "y", "x", "c")


def dot(a, b, ca=1, cb=0):
    return lax.dot_general(a, b, (((ca,), (cb,)), ((), ())), preferred_element_type=F32)


def mean_rows(v):
    return jnp.sum(v, axis=-1, keepdims=True) * (1.0 / v.shape[-1])


def lane_of(rows):
    return lax.broadcasted_iota(jnp.int32, (rows, LANES), 1)


def turned(t, low):
    return jnp.where(low, pltpu.roll(t, LANES - HD // 2, 1), pltpu.roll(t, HD // 2, 1))


def swap(t):
    return pltpu.roll(t, HD, 1)


def gain_rows(w_ref):
    cols = w_ref[:, 3 * D :].astype(F32).T
    return cols[E : E + 1, :], cols[E + 1 : E + 2, :]


def bias_of(lens_ref, micro):
    row = lax.broadcasted_iota(jnp.int32, (MB, MB), 0)
    col = lax.broadcasted_iota(jnp.int32, (MB, MB), 1)
    start = jnp.zeros((MB, MB), jnp.int32)
    end = jnp.int32(0)
    for s in range(3):
        end = end + lens_ref[micro, s]
        start = jnp.where(row >= end, end, start)
    return jnp.where((col >= start) & (col <= row), 0.0, NEG)


def split_pair(block, half):
    low = lane_of(block.shape[0]) < HD
    other = swap(block)
    here, there = (block, other) if half == 0 else (other, block)
    return jnp.concatenate(
        [jnp.where(low, here, 0.0), jnp.where(low, 0.0, there)], axis=0
    ).astype(BF)


def softmax_pair(score, bias):
    halves = []
    for h in range(2):
        s = score[:, h * MB : (h + 1) * MB] * 0.125 + bias
        e = jnp.exp(s - jnp.max(s, axis=1, keepdims=True))
        halves.append(e * (1.0 / jnp.sum(e, axis=1, keepdims=True)))
    return jnp.concatenate(halves, axis=1)


def attention_forward_kernel(
    micro, outer, place_ref, lens_ref, tok_ref, cot_ref, w_ref, cos_ref, sin_ref,
    nm_ref, q_ref, kv_ref, mixed_ref, resid_ref, weight_ref, *ordering,
):
    if not micro:
        ordered_ref, w_all, sems, out_sem = ordering
        share = D // outer // PLANE
        copies = []
        for p in range(PLANE):
            for s in range(outer):
                z = lax.rem(place_ref[1] + outer - s, outer)
                at = pl.ds(pl.multiple_of((z * PLANE + p) * share, share), share)
                block = w_ref.at[(p * outer + s) * share : (p * outer + s + 1) * share]
                copies.append(pltpu.make_async_copy(block, w_all.at[at], sems.at[p * outer + s]))
        for copy in copies:
            copy.start()
        for copy in copies:
            copy.wait()
        write = pltpu.make_async_copy(w_all, ordered_ref, out_sem)
        write.start()
        w_ref = w_all
    gain_in, gain_mid = gain_rows(w_ref)
    x = tok_ref[...].astype(F32)
    normed = (x * lax.rsqrt(mean_rows(x * x) + EPS) * gain_in).astype(BF)
    q_lin = dot(normed, w_ref[:, :D])
    kv_lin = dot(normed, w_ref[:, D : 2 * D])
    cosine, sine = cos_ref[...], sin_ref[...]
    low = (lane_of(MB) % HD) < HD // 2
    bias = bias_of(lens_ref, micro)
    mixed = []
    for pair in range(GROUPS // 2):
        lanes = slice(pair * LANES, (pair + 1) * LANES)
        k_pair = kv_lin[:, lanes]
        k_pair = k_pair * cosine + turned(k_pair, low) * sine
        v_pair = kv_lin[:, D // 2 + pair * LANES : D // 2 + (pair + 1) * LANES]
        kv_ref[:, lanes] = k_pair.astype(BF)
        kv_ref[:, D // 2 + pair * LANES : D // 2 + (pair + 1) * LANES] = v_pair.astype(BF)
        for half in range(2):
            group = 2 * pair + half
            q = q_lin[:, group * LANES : (group + 1) * LANES]
            q = (q * cosine + turned(q, low) * sine).astype(BF)
            q_ref[:, group * LANES : (group + 1) * LANES] = q
            score = dot(q, split_pair(k_pair, half), 1, 1)
            weight = softmax_pair(score, bias).astype(BF)
            weight_ref[:, group * 2 * MB : (group + 1) * 2 * MB] = weight
            mixed.append(dot(weight, split_pair(v_pair, half)).astype(BF))
    mixed = jnp.concatenate(mixed, axis=1)
    mixed_ref[...] = mixed
    resid = x + dot(mixed, w_ref[:, 2 * D : 3 * D])
    resid_ref[...] = resid
    nm_ref[:, -D:] = (resid * lax.rsqrt(mean_rows(resid * resid) + EPS) * gain_mid).astype(BF)
    if micro:
        nm_ref[:, :DMID] = cot_ref[...]
    else:
        write.wait()


def masked_gates(logits, routed):
    top = jnp.max(jnp.where(routed, logits, NEG), axis=1, keepdims=True)
    e = jnp.where(routed, jnp.exp(jnp.minimum(logits - top, 0.0)), 0.0)
    return e * (1.0 / jnp.sum(e, axis=1, keepdims=True))


def plane_back(place_ref, s, outer, rows):
    z = lax.rem(place_ref[1] + outer - s, outer)
    return pl.ds(pl.multiple_of(z * rows, rows), rows)


def expert_kernel(outer, micro, e, *refs):
    refs = list(refs)
    take = lambda k: [refs.pop(0) for _ in range(k)]
    place_ref, *peers = take(3 if micro else 5)
    wr_ref = take(1)[0]
    homes = take(outer)
    partial_ref = take(1)[0] if e else None
    carried = take(2) if micro else []
    out_ref = take(1)[0]
    dmid_refs = take(2) if micro and e else []
    grads = take(outer) if micro else []
    acc_gu, acc_dn, w_gu, w_dn, sems = take(5)
    old_gu, old_dn = take(2) if micro else (None, None)
    step = pl.program_id(0)
    up_rows, down_rows = D // outer, FF // outer

    def old_copies():
        return [
            pltpu.make_async_copy(source, target, sems.at[outer, k])
            for k, (source, target) in enumerate(zip(carried, (old_gu, old_dn)))
        ]

    @pl.when(step == 0)
    def _():
        copies = []
        for s in range(outer):
            copies += [
                pltpu.make_async_copy(
                    homes[s].at[:up_rows], w_gu.at[plane_back(place_ref, s, outer, up_rows)], sems.at[s, 0]
                ),
                pltpu.make_async_copy(
                    homes[s].at[up_rows:], w_dn.at[plane_back(place_ref, s, outer, down_rows)], sems.at[s, 1]
                ),
            ]
        for copy in copies + (old_copies() if micro else []):
            copy.start()
        acc_gu[...] = jnp.zeros_like(acc_gu)
        acc_dn[...] = jnp.zeros_like(acc_dn)
        for copy in copies:
            copy.wait()

    cots, nms = (peers, peers) if micro else (peers[:2], peers[2:])
    nm = jnp.concatenate([ref[:, -D:] for ref in nms], axis=0)
    cot = jnp.concatenate([ref[:, :D] for ref in cots], axis=0)
    hot = jnp.concatenate([ref[:, D:DMID] for ref in cots], axis=0).astype(F32)
    lane = lane_of(nm.shape[0])
    expert = place_ref[0] * OWN + e
    if e:
        handed = partial_ref[:, D:DMID].astype(F32)
        mine = (lane == expert + 2 * E) | (lane == expert + 3 * E)
        combine = jnp.sum(jnp.where(mine, handed, 0.0), axis=1, keepdims=True)
    else:
        gates = masked_gates(dot(nm, wr_ref[...]), hot > 0.5)
        combine = jnp.sum(jnp.where(lane == expert, gates, 0.0), axis=1, keepdims=True)
    gateup = dot(nm, w_gu[...])
    gate, up = gateup[:, :FF], gateup[:, FF:]
    s = 1.0 / (1.0 + jnp.exp(-gate))
    silu = gate * s
    act = silu * up
    d_plain = dot(cot, w_dn[...], 1, 1)
    d_combine = jnp.sum(act * d_plain, axis=1, keepdims=True)
    act = (act * combine).astype(BF)
    out = dot(act, w_dn[...])
    d_act = d_plain * combine
    d_gateup = jnp.concatenate(
        [(d_act * up * (s * (1.0 + gate * (1.0 - s)))).astype(BF), (d_act * silu).astype(BF)], axis=1
    )
    d_mid = dot(d_gateup, w_gu[...], 1, 1)
    acc_gu[...] += dot(nm, d_gateup, 0, 0)
    acc_dn[...] += dot(act, cot, 0, 0)
    high = d_combine.astype(BF).astype(F32)
    extra = jnp.where(lane == expert, high, 0.0) + jnp.where(lane == expert + E, d_combine - high, 0.0)
    if e:
        d_mid = d_mid + partial_ref[:, :D].astype(F32)
        extra = extra + jnp.where(lane < 2 * E, handed, 0.0)
        out = out + partial_ref[:, DMID:].astype(F32)
    else:
        high = gates.astype(BF).astype(F32)
        extra = extra + pltpu.roll(high, 2 * E, 1) + pltpu.roll(gates - high, 3 * E, 1)
    d_mid = jnp.concatenate([d_mid.astype(BF), extra.astype(BF)], axis=1)
    out = out.astype(BF)
    if not e:
        out_ref[:, :DMID] = d_mid
        out_ref[:, DMID:] = out
    else:
        core = lax.rem(place_ref[0], 2)
        for half in range(2):
            part = slice(half * MB, (half + 1) * MB)
            at = pl.ds(pl.multiple_of((core if half == 0 else 1 - core) * MB, MB), MB)
            if micro:
                out_ref[at, :] = out[part]
                dmid_refs[half][...] = d_mid[part]
            else:
                out_ref[at, :DMID] = d_mid[part]
                out_ref[at, DMID:] = out[part]

    if micro:

        @pl.when(step == pl.num_programs(0) - 1)
        def _():
            for copy in old_copies():
                copy.wait()
            for s in range(outer):
                at = plane_back(place_ref, s, outer, up_rows)
                grads[s][:up_rows] = (acc_gu[at] + old_gu[at]).astype(BF)
                at = plane_back(place_ref, s, outer, down_rows)
                grads[s][up_rows:] = (acc_dn[at] + old_dn[at]).astype(BF)


def join_pair(a0, b0, a1, b1, low):
    return jnp.where(low, a0, b1) + swap(jnp.where(low, a1, b0))


def attention_backward_kernel(outer, last, *refs):
    refs = list(refs)
    take = lambda k: [refs.pop(0) for _ in range(k)]
    place_ref = take(1)[0]
    (tok_ref, cot_ref, nm_ref, q_ref, kv_ref, mixed_ref, resid_ref, weight_ref, dmid_ref, w_ref, cos_ref, sin_ref) = take(12)
    old = take(8) if last else []
    rows_ref = take(1)[0]
    kept = take(2 if last else 6)
    gain_in, gain_mid = gain_rows(w_ref)
    lane = lane_of(MB)
    cot = cot_ref[:, :D].astype(F32)
    resid = resid_ref[...]
    nm = nm_ref[:, -D:]
    w_small = w_ref[:, 3 * D :]
    gates = masked_gates(dot(nm, w_small), cot_ref[:, D:].astype(F32) > 0.5)
    pieces = dmid_ref[:, D:].astype(F32)
    d_gates = pieces + pltpu.roll(pieces, LANES - E, 1)
    d_logits = gates * (d_gates - jnp.sum(gates * d_gates, axis=1, keepdims=True))
    d_logits = jnp.where(lane < E, d_logits, 0.0).astype(BF)
    d_mid = dmid_ref[:, :D].astype(F32) + dot(d_logits, w_small, 1, 1)
    inverse = lax.rsqrt(mean_rows(resid * resid) + EPS)
    u = d_mid * gain_mid
    d_resid = cot + inverse * u - resid * (inverse * inverse * inverse) * mean_rows(u * resid)
    gain_mid_grad = jnp.sum(d_mid * resid * inverse, axis=0, keepdims=True)
    d_branch = d_resid.astype(BF)
    both = lambda k, value: jnp.concatenate([old[k][...], value], axis=0)
    leaving = []

    def leave(k, part):
        grad_ref, sems = refs
        share = D // outer // PLANE
        for s in range(outer):
            z = lax.rem(place_ref[1] + s, outer)
            for q in range(PLANE // 2):
                for other in range(2):
                    device = lax.bitwise_xor(place_ref[0], 2 * q + other)
                    at = pl.ds(pl.multiple_of((z * PLANE + device) * share, share), share)
                    sem = sems.at[k, s * PLANE + 2 * q + other]
                    copy = pltpu.make_async_copy(grad_ref.at[at, part], kept[other].at[s, q, :, part], sem)
                    copy.start()
                    leaving.append(copy)

    if last:
        refs[0][:, 2 * D : 3 * D] = dot(both(6, mixed_ref[...]), both(3, d_branch), 0, 0).astype(BF)
        leave(0, slice(2 * D, 3 * D))
    d_mixed = dot(d_branch, w_ref[:, 2 * D : 3 * D], 1, 1).astype(BF)

    cosine, sine = cos_ref[...], sin_ref[...]
    low = (lane % HD) < HD // 2
    head_low = lane < HD
    d_q, d_k, d_v = [], [], []
    for pair in range(GROUPS // 2):
        k_pair = kv_ref[:, pair * LANES : (pair + 1) * LANES].astype(F32)
        v_pair = kv_ref[:, D // 2 + pair * LANES : D // 2 + (pair + 1) * LANES].astype(F32)
        keys, values = [], []
        for half in range(2):
            group = 2 * pair + half
            q = q_ref[:, group * LANES : (group + 1) * LANES]
            dm = d_mixed[:, group * LANES : (group + 1) * LANES]
            k_two = split_pair(k_pair, half)
            weight = weight_ref[:, group * 2 * MB : (group + 1) * 2 * MB]
            p = weight.astype(F32)
            d_weight = dot(dm, split_pair(v_pair, half), 1, 1)
            scored = p * d_weight
            d_score = []
            for h in range(2):
                part = slice(h * MB, (h + 1) * MB)
                total = jnp.sum(scored[:, part], axis=1, keepdims=True)
                d_score.append((p[:, part] * (d_weight[:, part] - total)).astype(BF))
            d_score = jnp.concatenate(d_score, axis=1)
            d_query = dot(d_score, k_two) * 0.125
            d_q.append((d_query * cosine - turned(d_query, low) * sine).astype(BF))
            d_key = dot(d_score, q, 0, 0) * 0.125
            d_value = dot(weight, dm, 0, 0)
            keys += [d_key[:MB], d_key[MB:]]
            values += [d_value[:MB], d_value[MB:]]
        d_key = join_pair(*keys, head_low)
        d_k.append((d_key * cosine - turned(d_key, low) * sine).astype(BF))
        d_v.append(join_pair(*values, head_low).astype(BF))
    d_q = jnp.concatenate(d_q, axis=1)
    d_kv = jnp.concatenate(d_k + d_v, axis=1)

    x = tok_ref[...].astype(F32)
    inverse = lax.rsqrt(mean_rows(x * x) + EPS)
    normed = (x * inverse * gain_in).astype(BF)
    if last:
        normed_two = both(0, normed)
        refs[0][:, : D] = dot(normed_two, both(1, d_q), 0, 0).astype(BF)
        refs[0][:, D : 2 * D] = dot(normed_two, both(2, d_kv), 0, 0).astype(BF)
        leave(1, slice(0, 2 * D))
    d_in = dot(d_q, w_ref[:, :D], 1, 1) + dot(d_kv, w_ref[:, D : 2 * D], 1, 1)
    v = d_in * gain_in
    rows_ref[...] = d_resid + inverse * v - x * (inverse * inverse * inverse) * mean_rows(v * x)
    gain_in_grad = jnp.sum(d_in * x * inverse, axis=0, keepdims=True)
    gains = jnp.concatenate([gain_in_grad, gain_mid_grad, jnp.zeros((6, D), F32)], axis=0)
    if not last:
        for ref, value in zip(kept, (normed, d_q, d_kv, d_branch, d_logits, gains)):
            ref[...] = value
        return
    gains = jnp.concatenate([jnp.zeros((E, D), F32), gains + old[5][...], jnp.zeros((LANES - E - 8, D), F32)], axis=0)
    refs[0][:, 3 * D :] = (dot(both(7, nm), both(4, d_logits), 0, 0) + gains.T).astype(BF)
    leave(2, slice(3 * D, WIDE))
    for copy in leaving:
        copy.wait()


def blk(shape, index, buffers=None):
    if buffers is None:
        return pl.BlockSpec(shape, index)
    return pl.BlockSpec(shape, index, pipeline_mode=pl.Buffered(buffers))


def kernel_params(mib=58):
    return pltpu.CompilerParams(dimension_semantics=("arbitrary",), vmem_limit_bytes=mib << 20)


def takes(us):
    return pl.CostEstimate(flops=int(us * 1.15e9), bytes_accessed=1 << 20, transcendentals=0)


def shaped(rows, width, kind=BF):
    return jax.ShapeDtypeStruct((rows, width), kind)


def own_rows(width, micro=0):
    return blk((MB, width), lambda i, *_: (micro, 0))


def whole(shape):
    return blk(shape, lambda i, *_: (0,) * len(shape), 1)


def attention_forward(micro, outer, place, lengths, tokens, cot, packed, cosine, sine):
    width = DMID + D if micro else D
    any_ref = pl.BlockSpec(memory_space=pl.ANY)
    return pl.pallas_call(
        functools.partial(attention_forward_kernel, micro, outer),
        grid_spec=pltpu.PrefetchScalarGridSpec(
            num_scalar_prefetch=2,
            grid=(1,),
            in_specs=[own_rows(D, micro), own_rows(DMID, micro), whole((D, WIDE)) if micro else any_ref]
            + [own_rows(LANES, micro)] * 2,
            out_specs=[own_rows(width)] + [own_rows(D)] * 4 + [own_rows(D * 4)] + ([] if micro else [any_ref]),
            scratch_shapes=[]
            if micro
            else [pltpu.VMEM((D, WIDE), BF), pltpu.SemaphoreType.DMA((PLANE * outer,)), pltpu.SemaphoreType.DMA],
        ),
        out_shape=[shaped(MB, width)]
        + [shaped(MB, D)] * 3
        + [shaped(MB, D, F32), shaped(MB, D * 4)]
        + ([] if micro else [shaped(D, WIDE)]),
        compiler_params=kernel_params(),
        cost_estimate=takes(12),
        name=f"attention_forward_{micro}",
    )(place, lengths, tokens, cot, packed, cosine, sine)


def experts(micro, e, place, rows, packed, homes, carried=(), partial=()):
    outer = len(homes)
    wide = DMID + D
    any_ref = pl.BlockSpec(memory_space=pl.ANY)
    shape = jax.ShapeDtypeStruct

    def peer(k, width):
        return blk((MB, width), lambda i, place, *_: (lax.bitwise_xor(place[0], 2 * i + k), 0))

    near = blk((MB, DMID), lambda i, *_: (i, 0))
    pair = blk((2 * MB, wide), lambda i, *_: (i, 0))
    home = shape(homes[0].shape, BF)
    acc = [shape((D, 2 * FF), F32), shape((FF, D), F32)]
    in_specs = [peer(0, wide), peer(1, wide)] if micro else [near, near, peer(0, D), peer(1, D)]
    in_specs += [blk((D, LANES), lambda i, *_: (0, 3 * D // LANES), 1)]
    in_specs += [any_ref] * outer + [pair] * len(partial) + [any_ref] * len(carried)
    scratch = [
        pltpu.VMEM((D, 2 * FF), BF),
        pltpu.VMEM((FF, D), BF),
        pltpu.SemaphoreType.DMA((outer + 1, 2)),
    ]
    if not e:
        out_specs, out_shape = [pair], [shaped(PLANE * MB, wide)]
    else:
        width = D if micro else wide
        out_specs = [blk((2 * MB, width), lambda i, place, *_: (lax.bitwise_xor(place[0] // 2, i), 0))]
        out_shape = [shaped(PLANE * MB, width)]
        if micro:
            out_specs += [near, near]
            out_shape += [shaped(PLANE // 2 * MB, DMID)] * 2
    if micro:
        out_specs += [whole(home.shape)] * outer
        out_shape += [home] * outer
        scratch = [pltpu.VMEM(a.shape, F32) for a in acc] + scratch + [pltpu.VMEM(a.shape, F32) for a in acc]
    else:
        out_specs += [whole(a.shape) for a in acc]
        out_shape += acc
    return pl.pallas_call(
        functools.partial(expert_kernel, outer, micro, e),
        grid_spec=pltpu.PrefetchScalarGridSpec(
            num_scalar_prefetch=1,
            grid=(PLANE // 2,),
            in_specs=in_specs,
            out_specs=out_specs,
            scratch_shapes=scratch,
        ),
        out_shape=out_shape,
        compiler_params=kernel_params(),
        cost_estimate=takes(28),
        name=f"experts_{micro}_{e}",
    )(place, *rows, packed, *homes, *partial, *carried)


def attention_backward(micro, outer, place, tokens, cot, saved, d_mid, packed, cosine, sine, old):
    last = old is not None
    any_ref = pl.BlockSpec(memory_space=pl.ANY)
    in_specs = [own_rows(D, micro), own_rows(DMID, micro)] + [own_rows(v.shape[1]) for v in saved]
    in_specs += [own_rows(DMID), whole((D, WIDE)), own_rows(LANES, micro), own_rows(LANES, micro)]
    args = [tokens, cot, *saved, d_mid, packed, cosine, sine]
    kept = [shaped(MB, D)] * 4 + [shaped(MB, LANES), shaped(8, D, F32)]
    kept_specs = [whole(a.shape) for a in kept]
    scratch = []
    if last:
        args += old
        in_specs += [whole(a.shape) for a in old]
        share = D // outer // PLANE
        kept = [jax.ShapeDtypeStruct((outer, PLANE // 2, share, WIDE), BF)] * 2
        kept_specs = [any_ref] * 2
        scratch = [pltpu.VMEM((D, WIDE), BF), pltpu.SemaphoreType.DMA((3, outer * PLANE))]
    return pl.pallas_call(
        functools.partial(attention_backward_kernel, outer, last),
        grid_spec=pltpu.PrefetchScalarGridSpec(
            num_scalar_prefetch=1,
            grid=(1,),
            in_specs=in_specs,
            out_specs=[own_rows(D)] + kept_specs,
            scratch_shapes=scratch,
        ),
        out_shape=[shaped(MB, D, F32)] + kept,
        compiler_params=kernel_params(),
        cost_estimate=takes(18 if last else 13),
        name=f"attention_backward_{micro}",
    )(place, *args)


def rope_tables(lengths):
    ends = jnp.stack([jnp.sum(lengths[:, : s + 1], axis=1) for s in range(lengths.shape[1] - 1)], axis=1)
    index = jnp.arange(MB, dtype=jnp.int32)
    start = jnp.max(jnp.where(ends[:, None, :] <= index[None, :, None], ends[:, None, :], 0), axis=2)
    position = (index[None, :] - start).astype(F32).reshape(-1)
    lane = jnp.arange(LANES, dtype=jnp.int32)
    freq = jnp.exp(-((2 * (lane % (HD // 2))).astype(F32) / HD) * jnp.log(10000.0))
    angle = position[:, None] * freq[None, :]
    sign = jnp.where(lane % HD < HD // 2, -1.0, 1.0)
    return jnp.cos(angle), jnp.sin(angle) * sign[None, :]


def gather(v, axes):
    return lax.all_gather(v, axes, axis=0, tiled=True)


def scatter_sum(v, axes, dim=0):
    return lax.psum_scatter(v, axes, scatter_dimension=dim, tiled=True)


def tie(*values):
    return lax.optimization_barrier(values)


def after(v, *others):
    return tie(v, *others)[0]


def across(v, axis):
    return lax.ppermute(v, axis, [(0, 1), (1, 0)])


def onward(v, steps=1):
    count = lax.axis_size("z")
    return lax.ppermute(v, "z", [(i, (i + steps) % count) for i in range(count)])


def plus(a, b):
    return (a.astype(F32) + b.astype(F32)).astype(BF)


def sum_weights(same, other, beside):
    outer = same.shape[0]
    cut = same.shape[-1] // 2 // LANES * LANES

    def both(stage, *values):
        start, took = beside[stage]
        *values, extra = tie(*values, start())
        took(extra)
        return values

    total = plus(same, across(other, "c"))
    first, second = total[..., :cut], total[..., cut:]
    got_x, got_y = both(0, across(first[:, 1::2], "x"), across(second[:, 2:], "y"))
    first, second = plus(first[:, ::2], got_x), plus(second[:, :2], got_y)
    got_y, got_x = both(1, across(first[:, 1], "y"), across(second[:, 1], "x"))
    total = jnp.concatenate([plus(first[:, 0], got_y), plus(second[:, 0], got_x)], axis=-1)
    terms = [total[0]] + [onward(total[s], s) for s in range(1, outer)]
    return sum(term.astype(F32) for term in terms)


def sum_to_owners(same, other, early, late):
    total = plus(same, across(other, "c"))
    total = total.reshape(4, 2, MB // 2, -1)
    first = [total[i, 0] for i in range(4)]
    second = [total[i, 1] for i in range(4)]
    got_x = across(jnp.stack([first[1], first[3]]), "x")
    got_y = across(jnp.stack([second[2], second[3]]), "y")
    got_x, got_y, early = tie(got_x, got_y, early)
    last_x, last_y = across(plus(second[1], got_y[1]), "x"), across(plus(first[2], got_x[1]), "y")
    last_x, last_y, late = tie(last_x, last_y, late)
    return jnp.concatenate(
        [
            (first[0].astype(F32) + got_x[0].astype(F32) + last_y.astype(F32)).astype(BF),
            (second[0].astype(F32) + got_y[0].astype(F32) + last_x.astype(F32)).astype(BF),
        ],
        axis=0,
    ), early, late


def shards(tokens, cotangent, lengths, routes, attn_gain, w_query, w_keyval, w_out, moe_gain, w_router, w_gateup, w_down):
    share = w_query.shape[0]
    outer = lax.axis_size("z")
    place = jnp.stack([lax.axis_index(PLANE_AXES), lax.axis_index("z")]).astype(jnp.int32)

    small = jnp.concatenate(
        [w_router, attn_gain[:, None], moe_gain[:, None], jnp.zeros((share, LANES - E - 2), BF)], axis=1
    )
    own = jnp.concatenate([w_query, w_keyval, w_out, small], axis=1)
    pieces = [own] + [onward(own, s) for s in range(1, outer)]
    sent = jnp.concatenate([w_gateup, w_down], axis=1)
    got = lax.all_to_all(
        sent.reshape(PLANE, OWN, *sent.shape[1:]), PLANE_AXES, split_axis=0, concat_axis=0, tiled=True
    )
    homes = [
        [jnp.concatenate([got[:, e, :share].reshape(-1, D), got[:, e, share:].reshape(-1, D)], axis=0)]
        for e in range(OWN)
    ]
    *pieces, homes[0][0], homes[1][0] = tie(*pieces, homes[0][0], homes[1][0])
    packed = gather(jnp.concatenate(pieces, axis=0), PLANE_AXES)

    def ring(e, count=1):
        for _ in range(count):
            homes[e].append(onward(homes[e][-1]))
        return homes[e][-1]

    hot = jnp.sum((routes[:, :, None] == jnp.arange(LANES, dtype=jnp.int32)[None, None, :]).astype(F32), axis=1)
    cot = jnp.concatenate([cotangent, hot.astype(BF)], axis=1)
    cosine, sine = rope_tables(lengths)

    packed, homes[0][-1] = tie(packed, ring(0, outer - 2))
    cot_0 = after(cot[:MB], homes[0][-1])
    from_x, from_y = across(cot_0, "x"), across(cot_0, "y")
    *saved_0, packed = attention_forward(0, outer, place, lengths, tokens, cot, packed, cosine, sine)
    nm_0, from_x, from_y, homes[0][-1] = tie(saved_0[0], from_x, from_y, ring(0))
    nm_0 = gather(nm_0, PLANE_AXES)
    corner_a, corner_b = across(from_x[: MB // 2], "y"), across(from_y[MB // 2 :], "x")
    packed, corner_a, corner_b, homes[1][-1] = tie(packed, corner_a, corner_b, ring(1, max(outer - 3, 0)))
    cot_same = jnp.concatenate([cot_0, from_x, from_y, corner_a, corner_b], axis=0)
    cot_other = across(cot_same, "c")
    saved_1 = attention_forward(1, outer, place, lengths, tokens, cot, packed, cosine, sine)
    nm_1, cot_other, homes[1][-1] = tie(saved_1[0], cot_other, ring(1))
    nm_1 = gather(nm_1, PLANE_AXES)
    ring(1, outer - len(homes[1]))

    rows = [cot_same, cot_other, nm_0, nm_0]
    partial, *carried_a = experts(0, 0, place, rows, packed, homes[0])
    both_0, *carried_b = experts(0, 1, place, rows, packed, homes[1], partial=[partial])
    rows = [nm_1, nm_1]
    partial, *turns_a = experts(1, 0, place, rows, packed, homes[0], carried_a)
    out_1, same_1, other_1, *turns_b = experts(1, 1, place, rows, packed, homes[1], carried_b, [partial])

    turns = [turns_a, turns_b]
    moved = [turns_a[1], turns_b[1]]

    def pass_on(e, first, last):
        for s in range(first, last):
            moved[e] = onward(moved[e] if s == 1 else plus(turns[e][s], moved[e]))
        return moved[e]

    other_1, moved[0] = tie(other_1, pass_on(0, 1, 2))
    both_0 = scatter_sum(both_0, PLANE_AXES)
    rows_0, *old = attention_backward(0, outer, place, tokens, cot, saved_0, both_0, packed, cosine, sine, None)
    old = old + [saved_0[3], saved_0[0]]
    early = rows_0, pass_on(0, 2, outer - 1)
    moved[1] = after(moved[1], rows_0)
    d_mid_1, (rows_0, moved[0]), moved[1] = sum_to_owners(same_1, other_1, early, pass_on(1, 1, outer - 2))
    summed_0, out_1 = both_0[:, DMID:], scatter_sum(out_1, PLANE_AXES)
    d_mid_1, moved[1] = tie(d_mid_1, moved[1])
    following = plus(turns[1][outer - 2], moved[1])
    d_mid_1, following = tie(d_mid_1, following)
    rows_1, grads, grads_other = attention_backward(1, outer, place, tokens, cot, saved_1, d_mid_1, packed, cosine, sine, old)
    grads, grads_other, moved[0], out_1 = tie(grads, grads_other, pass_on(0, outer - 1, outer), out_1)
    out_sums = summed_0, out_1
    output = [(saved[4] + part.astype(F32)).astype(BF) for saved, part in zip((saved_0, saved_1), out_sums)]
    beside = (
        (lambda: onward(following), lambda v: moved.__setitem__(1, v)),
        (lambda: pass_on(1, outer - 1, outer), lambda v: moved.__setitem__(1, v)),
    )
    grads = sum_weights(grads, grads_other, beside)
    home = jnp.stack([plus(turns[e][0], moved[e]) for e in range(OWN)])
    up, down = home[:, : PLANE * share], home[:, PLANE * share :]
    home = jnp.concatenate(
        [up.reshape(OWN, PLANE, share, D), down.reshape(OWN, PLANE, share // 2, D)], axis=2
    ).transpose(1, 0, 2, 3)
    home = lax.all_to_all(home, PLANE_AXES, split_axis=0, concat_axis=0, tiled=True)
    home = home.reshape(E, -1, D)
    return (
        jnp.concatenate(output, axis=0),
        jnp.concatenate([rows_0, rows_1], axis=0),
        grads[:, 3 * D + E],
        grads[:, :D],
        grads[:, D : 2 * D],
        grads[:, 2 * D : 3 * D],
        grads[:, 3 * D + E + 1],
        grads[:, 3 * D : 3 * D + E],
        home[:, :share].astype(F32),
        home[:, share:].astype(F32),
    )


def solution(mesh):
    count = mesh.shape["fsdp"]
    inner = Mesh(mesh.devices.reshape(count // PLANE, 2, 2, 2), ALL)
    row, vec, mid = P(ALL, None), P(ALL), P(None, ALL, None)
    return jax.shard_map(
        shards,
        mesh=inner,
        in_specs=(row, row, row, row, vec, row, row, row, vec, row, mid, mid),
        out_specs=(row, row, vec, row, row, row, vec, row, mid, mid),
        check_vma=False,
    )
```

```python
import functools

import jax
import jax.numpy as jnp
from jax import lax
from jax.experimental import pallas as pl
from jax.experimental.pallas import tpu as pltpu
from jax.sharding import Mesh, PartitionSpec as P

D = 1024
HD = 64
FF = 512
E = 16
MB = 256
GROUPS = 8
PLANE = 8
OWN = E // PLANE
LANES = 128
WIDE = 3 * D + LANES
DMID = D + LANES
EPS = 1e-05
NEG = -1e30

BF = jnp.bfloat16
F32 = jnp.float32
PLANE_AXES = ("y", "x", "c")
ALL = ("z", "y", "x", "c")


def dot(a, b, ca=1, cb=0):
    return lax.dot_general(a, b, (((ca,), (cb,)), ((), ())), preferred_element_type=F32)


def mean_rows(v):
    return jnp.sum(v, axis=-1, keepdims=True) * (1.0 / v.shape[-1])


def lane_of(rows):
    return lax.broadcasted_iota(jnp.int32, (rows, LANES), 1)


def turned(t, low):
    return jnp.where(low, pltpu.roll(t, LANES - HD // 2, 1), pltpu.roll(t, HD // 2, 1))


def swap(t):
    return pltpu.roll(t, HD, 1)


def gain_rows(w_ref):
    cols = w_ref[:, 3 * D :].astype(F32).T
    return cols[E : E + 1, :], cols[E + 1 : E + 2, :]


def bias_of(lens_ref, micro):
    row = lax.broadcasted_iota(jnp.int32, (MB, MB), 0)
    col = lax.broadcasted_iota(jnp.int32, (MB, MB), 1)
    start = jnp.zeros((MB, MB), jnp.int32)
    end = jnp.int32(0)
    for s in range(3):
        end = end + lens_ref[micro, s]
        start = jnp.where(row >= end, end, start)
    return jnp.where((col >= start) & (col <= row), 0.0, NEG)


def split_pair(block, half):
    low = lane_of(block.shape[0]) < HD
    other = swap(block)
    here, there = (block, other) if half == 0 else (other, block)
    return jnp.concatenate(
        [jnp.where(low, here, 0.0), jnp.where(low, 0.0, there)], axis=0
    ).astype(BF)


def softmax_pair(score, bias):
    halves = []
    for h in range(2):
        s = score[:, h * MB : (h + 1) * MB] * 0.125 + bias
        e = jnp.exp(s - jnp.max(s, axis=1, keepdims=True))
        halves.append(e * (1.0 / jnp.sum(e, axis=1, keepdims=True)))
    return jnp.concatenate(halves, axis=1)


def attention_forward_kernel(
    micro, outer, place_ref, lens_ref, tok_ref, cot_ref, w_ref, cos_ref, sin_ref,
    nm_ref, q_ref, kv_ref, mixed_ref, resid_ref, weight_ref, *ordering,
):
    if not micro:
        ordered_ref, w_all, sems, out_sem = ordering
        share = D // outer // PLANE
        copies = []
        for p in range(PLANE):
            for s in range(outer):
                z = lax.rem(place_ref[1] + outer - s, outer)
                at = pl.ds(pl.multiple_of((z * PLANE + p) * share, share), share)
                block = w_ref.at[(p * outer + s) * share : (p * outer + s + 1) * share]
                copies.append(pltpu.make_async_copy(block, w_all.at[at], sems.at[p * outer + s]))
        for copy in copies:
            copy.start()
        for copy in copies:
            copy.wait()
        write = pltpu.make_async_copy(w_all, ordered_ref, out_sem)
        write.start()
        w_ref = w_all
    gain_in, gain_mid = gain_rows(w_ref)
    x = tok_ref[...].astype(F32)
    normed = (x * lax.rsqrt(mean_rows(x * x) + EPS) * gain_in).astype(BF)
    q_lin = dot(normed, w_ref[:, :D])
    kv_lin = dot(normed, w_ref[:, D : 2 * D])
    cosine, sine = cos_ref[...], sin_ref[...]
    low = (lane_of(MB) % HD) < HD // 2
    bias = bias_of(lens_ref, micro)
    mixed = []
    for pair in range(GROUPS // 2):
        lanes = slice(pair * LANES, (pair + 1) * LANES)
        k_pair = kv_lin[:, lanes]
        k_pair = k_pair * cosine + turned(k_pair, low) * sine
        v_pair = kv_lin[:, D // 2 + pair * LANES : D // 2 + (pair + 1) * LANES]
        kv_ref[:, lanes] = k_pair.astype(BF)
        kv_ref[:, D // 2 + pair * LANES : D // 2 + (pair + 1) * LANES] = v_pair.astype(BF)
        for half in range(2):
            group = 2 * pair + half
            q = q_lin[:, group * LANES : (group + 1) * LANES]
            q = (q * cosine + turned(q, low) * sine).astype(BF)
            q_ref[:, group * LANES : (group + 1) * LANES] = q
            score = dot(q, split_pair(k_pair, half), 1, 1)
            weight = softmax_pair(score, bias).astype(BF)
            weight_ref[:, group * 2 * MB : (group + 1) * 2 * MB] = weight
            mixed.append(dot(weight, split_pair(v_pair, half)).astype(BF))
    mixed = jnp.concatenate(mixed, axis=1)
    mixed_ref[...] = mixed
    resid = x + dot(mixed, w_ref[:, 2 * D : 3 * D])
    resid_ref[...] = resid
    nm_ref[:, -D:] = (resid * lax.rsqrt(mean_rows(resid * resid) + EPS) * gain_mid).astype(BF)
    if micro:
        nm_ref[:, :DMID] = cot_ref[...]
    else:
        write.wait()


def masked_gates(logits, routed):
    top = jnp.max(jnp.where(routed, logits, NEG), axis=1, keepdims=True)
    e = jnp.where(routed, jnp.exp(jnp.minimum(logits - top, 0.0)), 0.0)
    return e * (1.0 / jnp.sum(e, axis=1, keepdims=True))


def plane_back(place_ref, s, outer, rows):
    z = lax.rem(place_ref[1] + outer - s, outer)
    return pl.ds(pl.multiple_of(z * rows, rows), rows)


def expert_kernel(outer, micro, e, *refs):
    refs = list(refs)
    take = lambda k: [refs.pop(0) for _ in range(k)]
    place_ref, *peers = take(3 if micro else 5)
    wr_ref = take(1)[0]
    homes = take(outer)
    partial_ref = take(1)[0] if e else None
    carried = take(2) if micro else []
    out_ref = take(1)[0]
    dmid_refs = take(2) if micro and e else []
    grads = take(outer) if micro else []
    acc_gu, acc_dn, w_gu, w_dn, sems = take(5)
    old_gu, old_dn = take(2) if micro else (None, None)
    step = pl.program_id(0)
    up_rows, down_rows = D // outer, FF // outer

    def old_copies():
        return [
            pltpu.make_async_copy(source, target, sems.at[outer, k])
            for k, (source, target) in enumerate(zip(carried, (old_gu, old_dn)))
        ]

    @pl.when(step == 0)
    def _():
        copies = []
        for s in range(outer):
            copies += [
                pltpu.make_async_copy(
                    homes[s].at[:up_rows], w_gu.at[plane_back(place_ref, s, outer, up_rows)], sems.at[s, 0]
                ),
                pltpu.make_async_copy(
                    homes[s].at[up_rows:], w_dn.at[plane_back(place_ref, s, outer, down_rows)], sems.at[s, 1]
                ),
            ]
        for copy in copies + (old_copies() if micro else []):
            copy.start()
        acc_gu[...] = jnp.zeros_like(acc_gu)
        acc_dn[...] = jnp.zeros_like(acc_dn)
        for copy in copies:
            copy.wait()

    cots, nms = (peers, peers) if micro else (peers[:2], peers[2:])
    nm = jnp.concatenate([ref[:, -D:] for ref in nms], axis=0)
    cot = jnp.concatenate([ref[:, :D] for ref in cots], axis=0)
    hot = jnp.concatenate([ref[:, D:DMID] for ref in cots], axis=0).astype(F32)
    lane = lane_of(nm.shape[0])
    expert = place_ref[0] * OWN + e
    if e:
        handed = partial_ref[:, D:DMID].astype(F32)
        mine = (lane == expert + 2 * E) | (lane == expert + 3 * E)
        combine = jnp.sum(jnp.where(mine, handed, 0.0), axis=1, keepdims=True)
    else:
        gates = masked_gates(dot(nm, wr_ref[...]), hot > 0.5)
        combine = jnp.sum(jnp.where(lane == expert, gates, 0.0), axis=1, keepdims=True)
    gateup = dot(nm, w_gu[...])
    gate, up = gateup[:, :FF], gateup[:, FF:]
    s = 1.0 / (1.0 + jnp.exp(-gate))
    silu = gate * s
    act = silu * up
    d_plain = dot(cot, w_dn[...], 1, 1)
    d_combine = jnp.sum(act * d_plain, axis=1, keepdims=True)
    act = (act * combine).astype(BF)
    out = dot(act, w_dn[...])
    d_act = d_plain * combine
    d_gateup = jnp.concatenate(
        [(d_act * up * (s * (1.0 + gate * (1.0 - s)))).astype(BF), (d_act * silu).astype(BF)], axis=1
    )
    d_mid = dot(d_gateup, w_gu[...], 1, 1)
    acc_gu[...] += dot(nm, d_gateup, 0, 0)
    acc_dn[...] += dot(act, cot, 0, 0)
    high = d_combine.astype(BF).astype(F32)
    extra = jnp.where(lane == expert, high, 0.0) + jnp.where(lane == expert + E, d_combine - high, 0.0)
    if e:
        d_mid = d_mid + partial_ref[:, :D].astype(F32)
        extra = extra + jnp.where(lane < 2 * E, handed, 0.0)
        out = out + partial_ref[:, DMID:].astype(F32)
    else:
        high = gates.astype(BF).astype(F32)
        extra = extra + pltpu.roll(high, 2 * E, 1) + pltpu.roll(gates - high, 3 * E, 1)
    d_mid = jnp.concatenate([d_mid.astype(BF), extra.astype(BF)], axis=1)
    out = out.astype(BF)
    if not e:
        out_ref[:, :DMID] = d_mid
        out_ref[:, DMID:] = out
    else:
        core = lax.rem(place_ref[0], 2)
        for half in range(2):
            part = slice(half * MB, (half + 1) * MB)
            at = pl.ds(pl.multiple_of((core if half == 0 else 1 - core) * MB, MB), MB)
            if micro:
                out_ref[at, :] = out[part]
                dmid_refs[half][...] = d_mid[part]
            else:
                out_ref[at, :DMID] = d_mid[part]
                out_ref[at, DMID:] = out[part]

    if micro:

        @pl.when(step == pl.num_programs(0) - 1)
        def _():
            for copy in old_copies():
                copy.wait()
            for s in range(outer):
                at = plane_back(place_ref, s, outer, up_rows)
                grads[s][:up_rows] = (acc_gu[at] + old_gu[at]).astype(BF)
                at = plane_back(place_ref, s, outer, down_rows)
                grads[s][up_rows:] = (acc_dn[at] + old_dn[at]).astype(BF)


def join_pair(a0, b0, a1, b1, low):
    return jnp.where(low, a0, b1) + swap(jnp.where(low, a1, b0))


def attention_backward_kernel(outer, last, *refs):
    refs = list(refs)
    take = lambda k: [refs.pop(0) for _ in range(k)]
    place_ref = take(1)[0]
    (tok_ref, cot_ref, nm_ref, q_ref, kv_ref, mixed_ref, resid_ref, weight_ref, dmid_ref, w_ref, cos_ref, sin_ref) = take(12)
    old = take(8) if last else []
    rows_ref = take(1)[0]
    kept = take(2 if last else 6)
    gain_in, gain_mid = gain_rows(w_ref)
    lane = lane_of(MB)
    cot = cot_ref[:, :D].astype(F32)
    resid = resid_ref[...]
    nm = nm_ref[:, -D:]
    w_small = w_ref[:, 3 * D :]
    gates = masked_gates(dot(nm, w_small), cot_ref[:, D:].astype(F32) > 0.5)
    pieces = dmid_ref[:, D:].astype(F32)
    d_gates = pieces + pltpu.roll(pieces, LANES - E, 1)
    d_logits = gates * (d_gates - jnp.sum(gates * d_gates, axis=1, keepdims=True))
    d_logits = jnp.where(lane < E, d_logits, 0.0).astype(BF)
    d_mid = dmid_ref[:, :D].astype(F32) + dot(d_logits, w_small, 1, 1)
    inverse = lax.rsqrt(mean_rows(resid * resid) + EPS)
    u = d_mid * gain_mid
    d_resid = cot + inverse * u - resid * (inverse * inverse * inverse) * mean_rows(u * resid)
    gain_mid_grad = jnp.sum(d_mid * resid * inverse, axis=0, keepdims=True)
    d_branch = d_resid.astype(BF)
    both = lambda k, value: jnp.concatenate([old[k][...], value], axis=0)
    leaving = []

    def leave(k, part):
        grad_ref, sems = refs
        share = D // outer // PLANE
        for s in range(outer):
            z = lax.rem(place_ref[1] + s, outer)
            for q in range(PLANE // 2):
                for other in range(2):
                    device = lax.bitwise_xor(place_ref[0], 2 * q + other)
                    at = pl.ds(pl.multiple_of((z * PLANE + device) * share, share), share)
                    sem = sems.at[k, s * PLANE + 2 * q + other]
                    copy = pltpu.make_async_copy(grad_ref.at[at, part], kept[other].at[s, q, :, part], sem)
                    copy.start()
                    leaving.append(copy)

    if last:
        refs[0][:, 2 * D : 3 * D] = dot(both(6, mixed_ref[...]), both(3, d_branch), 0, 0).astype(BF)
        leave(0, slice(2 * D, 3 * D))
    d_mixed = dot(d_branch, w_ref[:, 2 * D : 3 * D], 1, 1).astype(BF)

    cosine, sine = cos_ref[...], sin_ref[...]
    low = (lane % HD) < HD // 2
    head_low = lane < HD
    d_q, d_k, d_v = [], [], []
    for pair in range(GROUPS // 2):
        k_pair = kv_ref[:, pair * LANES : (pair + 1) * LANES].astype(F32)
        v_pair = kv_ref[:, D // 2 + pair * LANES : D // 2 + (pair + 1) * LANES].astype(F32)
        keys, values = [], []
        for half in range(2):
            group = 2 * pair + half
            q = q_ref[:, group * LANES : (group + 1) * LANES]
            dm = d_mixed[:, group * LANES : (group + 1) * LANES]
            k_two = split_pair(k_pair, half)
            weight = weight_ref[:, group * 2 * MB : (group + 1) * 2 * MB]
            p = weight.astype(F32)
            d_weight = dot(dm, split_pair(v_pair, half), 1, 1)
            scored = p * d_weight
            d_score = []
            for h in range(2):
                part = slice(h * MB, (h + 1) * MB)
                total = jnp.sum(scored[:, part], axis=1, keepdims=True)
                d_score.append((p[:, part] * (d_weight[:, part] - total)).astype(BF))
            d_score = jnp.concatenate(d_score, axis=1)
            d_query = dot(d_score, k_two) * 0.125
            d_q.append((d_query * cosine - turned(d_query, low) * sine).astype(BF))
            d_key = dot(d_score, q, 0, 0) * 0.125
            d_value = dot(weight, dm, 0, 0)
            keys += [d_key[:MB], d_key[MB:]]
            values += [d_value[:MB], d_value[MB:]]
        d_key = join_pair(*keys, head_low)
        d_k.append((d_key * cosine - turned(d_key, low) * sine).astype(BF))
        d_v.append(join_pair(*values, head_low).astype(BF))
    d_q = jnp.concatenate(d_q, axis=1)
    d_kv = jnp.concatenate(d_k + d_v, axis=1)

    x = tok_ref[...].astype(F32)
    inverse = lax.rsqrt(mean_rows(x * x) + EPS)
    normed = (x * inverse * gain_in).astype(BF)
    if last:
        normed_two = both(0, normed)
        refs[0][:, : D] = dot(normed_two, both(1, d_q), 0, 0).astype(BF)
        refs[0][:, D : 2 * D] = dot(normed_two, both(2, d_kv), 0, 0).astype(BF)
        leave(1, slice(0, 2 * D))
    d_in = dot(d_q, w_ref[:, :D], 1, 1) + dot(d_kv, w_ref[:, D : 2 * D], 1, 1)
    v = d_in * gain_in
    rows_ref[...] = d_resid + inverse * v - x * (inverse * inverse * inverse) * mean_rows(v * x)
    gain_in_grad = jnp.sum(d_in * x * inverse, axis=0, keepdims=True)
    gains = jnp.concatenate([gain_in_grad, gain_mid_grad, jnp.zeros((6, D), F32)], axis=0)
    if not last:
        for ref, value in zip(kept, (normed, d_q, d_kv, d_branch, d_logits, gains)):
            ref[...] = value
        return
    gains = jnp.concatenate([jnp.zeros((E, D), F32), gains + old[5][...], jnp.zeros((LANES - E - 8, D), F32)], axis=0)
    refs[0][:, 3 * D :] = (dot(both(7, nm), both(4, d_logits), 0, 0) + gains.T).astype(BF)
    leave(2, slice(3 * D, WIDE))
    for copy in leaving:
        copy.wait()


def blk(shape, index, buffers=None):
    if buffers is None:
        return pl.BlockSpec(shape, index)
    return pl.BlockSpec(shape, index, pipeline_mode=pl.Buffered(buffers))


def kernel_params(mib=58):
    return pltpu.CompilerParams(dimension_semantics=("arbitrary",), vmem_limit_bytes=mib << 20)


def takes(us):
    return pl.CostEstimate(flops=int(us * 1.15e9), bytes_accessed=1 << 20, transcendentals=0)


def shaped(rows, width, kind=BF):
    return jax.ShapeDtypeStruct((rows, width), kind)


def own_rows(width, micro=0):
    return blk((MB, width), lambda i, *_: (micro, 0))


def whole(shape):
    return blk(shape, lambda i, *_: (0,) * len(shape), 1)


def attention_forward(micro, outer, place, lengths, tokens, cot, packed, cosine, sine):
    width = DMID + D if micro else D
    any_ref = pl.BlockSpec(memory_space=pl.ANY)
    return pl.pallas_call(
        functools.partial(attention_forward_kernel, micro, outer),
        grid_spec=pltpu.PrefetchScalarGridSpec(
            num_scalar_prefetch=2,
            grid=(1,),
            in_specs=[own_rows(D, micro), own_rows(DMID, micro), whole((D, WIDE)) if micro else any_ref]
            + [own_rows(LANES, micro)] * 2,
            out_specs=[own_rows(width)] + [own_rows(D)] * 4 + [own_rows(D * 4)] + ([] if micro else [any_ref]),
            scratch_shapes=[]
            if micro
            else [pltpu.VMEM((D, WIDE), BF), pltpu.SemaphoreType.DMA((PLANE * outer,)), pltpu.SemaphoreType.DMA],
        ),
        out_shape=[shaped(MB, width)]
        + [shaped(MB, D)] * 3
        + [shaped(MB, D, F32), shaped(MB, D * 4)]
        + ([] if micro else [shaped(D, WIDE)]),
        compiler_params=kernel_params(),
        cost_estimate=takes(12),
        name=f"attention_forward_{micro}",
    )(place, lengths, tokens, cot, packed, cosine, sine)


def experts(micro, e, place, rows, packed, homes, carried=(), partial=()):
    outer = len(homes)
    wide = DMID + D
    any_ref = pl.BlockSpec(memory_space=pl.ANY)
    shape = jax.ShapeDtypeStruct

    def peer(k, width):
        return blk((MB, width), lambda i, place, *_: (lax.bitwise_xor(place[0], 2 * i + k), 0))

    near = blk((MB, DMID), lambda i, *_: (i, 0))
    pair = blk((2 * MB, wide), lambda i, *_: (i, 0))
    home = shape(homes[0].shape, BF)
    acc = [shape((D, 2 * FF), F32), shape((FF, D), F32)]
    in_specs = [peer(0, wide), peer(1, wide)] if micro else [near, near, peer(0, D), peer(1, D)]
    in_specs += [blk((D, LANES), lambda i, *_: (0, 3 * D // LANES), 1)]
    in_specs += [any_ref] * outer + [pair] * len(partial) + [any_ref] * len(carried)
    scratch = [
        pltpu.VMEM((D, 2 * FF), BF),
        pltpu.VMEM((FF, D), BF),
        pltpu.SemaphoreType.DMA((outer + 1, 2)),
    ]
    if not e:
        out_specs, out_shape = [pair], [shaped(PLANE * MB, wide)]
    else:
        width = D if micro else wide
        out_specs = [blk((2 * MB, width), lambda i, place, *_: (lax.bitwise_xor(place[0] // 2, i), 0))]
        out_shape = [shaped(PLANE * MB, width)]
        if micro:
            out_specs += [near, near]
            out_shape += [shaped(PLANE // 2 * MB, DMID)] * 2
    if micro:
        out_specs += [whole(home.shape)] * outer
        out_shape += [home] * outer
        scratch = [pltpu.VMEM(a.shape, F32) for a in acc] + scratch + [pltpu.VMEM(a.shape, F32) for a in acc]
    else:
        out_specs += [whole(a.shape) for a in acc]
        out_shape += acc
    return pl.pallas_call(
        functools.partial(expert_kernel, outer, micro, e),
        grid_spec=pltpu.PrefetchScalarGridSpec(
            num_scalar_prefetch=1,
            grid=(PLANE // 2,),
            in_specs=in_specs,
            out_specs=out_specs,
            scratch_shapes=scratch,
        ),
        out_shape=out_shape,
        compiler_params=kernel_params(),
        cost_estimate=takes(28),
        name=f"experts_{micro}_{e}",
    )(place, *rows, packed, *homes, *partial, *carried)


def attention_backward(micro, outer, place, tokens, cot, saved, d_mid, packed, cosine, sine, old):
    last = old is not None
    any_ref = pl.BlockSpec(memory_space=pl.ANY)
    in_specs = [own_rows(D, micro), own_rows(DMID, micro)] + [own_rows(v.shape[1]) for v in saved]
    in_specs += [own_rows(DMID), whole((D, WIDE)), own_rows(LANES, micro), own_rows(LANES, micro)]
    args = [tokens, cot, *saved, d_mid, packed, cosine, sine]
    kept = [shaped(MB, D)] * 4 + [shaped(MB, LANES), shaped(8, D, F32)]
    kept_specs = [whole(a.shape) for a in kept]
    scratch = []
    if last:
        args += old
        in_specs += [whole(a.shape) for a in old]
        share = D // outer // PLANE
        kept = [jax.ShapeDtypeStruct((outer, PLANE // 2, share, WIDE), BF)] * 2
        kept_specs = [any_ref] * 2
        scratch = [pltpu.VMEM((D, WIDE), BF), pltpu.SemaphoreType.DMA((3, outer * PLANE))]
    return pl.pallas_call(
        functools.partial(attention_backward_kernel, outer, last),
        grid_spec=pltpu.PrefetchScalarGridSpec(
            num_scalar_prefetch=1,
            grid=(1,),
            in_specs=in_specs,
            out_specs=[own_rows(D)] + kept_specs,
            scratch_shapes=scratch,
        ),
        out_shape=[shaped(MB, D, F32)] + kept,
        compiler_params=kernel_params(),
        cost_estimate=takes(18 if last else 13),
        name=f"attention_backward_{micro}",
    )(place, *args)


def rope_tables(lengths):
    ends = jnp.stack([jnp.sum(lengths[:, : s + 1], axis=1) for s in range(lengths.shape[1] - 1)], axis=1)
    index = jnp.arange(MB, dtype=jnp.int32)
    start = jnp.max(jnp.where(ends[:, None, :] <= index[None, :, None], ends[:, None, :], 0), axis=2)
    position = (index[None, :] - start).astype(F32).reshape(-1)
    lane = jnp.arange(LANES, dtype=jnp.int32)
    freq = jnp.exp(-((2 * (lane % (HD // 2))).astype(F32) / HD) * jnp.log(10000.0))
    angle = position[:, None] * freq[None, :]
    sign = jnp.where(lane % HD < HD // 2, -1.0, 1.0)
    return jnp.cos(angle), jnp.sin(angle) * sign[None, :]


def gather(v, axes):
    return lax.all_gather(v, axes, axis=0, tiled=True)


def scatter_sum(v, axes, dim=0):
    return lax.psum_scatter(v, axes, scatter_dimension=dim, tiled=True)


def tie(*values):
    return lax.optimization_barrier(values)


def after(v, *others):
    return tie(v, *others)[0]


def across(v, axis):
    return lax.ppermute(v, axis, [(0, 1), (1, 0)])


def onward(v, steps=1):
    count = lax.axis_size("z")
    return lax.ppermute(v, "z", [(i, (i + steps) % count) for i in range(count)])


def plus(a, b):
    return (a.astype(F32) + b.astype(F32)).astype(BF)


def sum_weights(same, other, beside):
    outer = same.shape[0]
    cut = same.shape[-1] // 2 // LANES * LANES

    def both(stage, *values):
        start, took = beside[stage]
        *values, extra = tie(*values, start())
        took(extra)
        return values

    total = plus(same, across(other, "c"))
    first, second = total[..., :cut], total[..., cut:]
    got_x, got_y = both(0, across(first[:, 1::2], "x"), across(second[:, 2:], "y"))
    first, second = plus(first[:, ::2], got_x), plus(second[:, :2], got_y)
    beside[1][1](beside[1][0]())
    got_y, got_x = across(first[:, 1], "y"), across(second[:, 1], "x")
    total = jnp.concatenate([plus(first[:, 0], got_y), plus(second[:, 0], got_x)], axis=-1)
    terms = [total[0]] + [onward(total[s], s) for s in range(1, outer)]
    return sum(term.astype(F32) for term in terms)


def sum_to_owners(same, other, early, late):
    total = plus(same, across(other, "c"))
    total = total.reshape(4, 2, MB // 2, -1)
    first = [total[i, 0] for i in range(4)]
    second = [total[i, 1] for i in range(4)]
    got_x = across(jnp.stack([first[1], first[3]]), "x")
    got_y = across(jnp.stack([second[2], second[3]]), "y")
    got_x, got_y, early = tie(got_x, got_y, early)
    last_x, last_y = across(plus(second[1], got_y[1]), "x"), across(plus(first[2], got_x[1]), "y")
    last_x, last_y, late = tie(last_x, last_y, late)
    return jnp.concatenate(
        [
            (first[0].astype(F32) + got_x[0].astype(F32) + last_y.astype(F32)).astype(BF),
            (second[0].astype(F32) + got_y[0].astype(F32) + last_x.astype(F32)).astype(BF),
        ],
        axis=0,
    ), early, late


def shards(tokens, cotangent, lengths, routes, attn_gain, w_query, w_keyval, w_out, moe_gain, w_router, w_gateup, w_down):
    share = w_query.shape[0]
    outer = lax.axis_size("z")
    place = jnp.stack([lax.axis_index(PLANE_AXES), lax.axis_index("z")]).astype(jnp.int32)

    small = jnp.concatenate(
        [w_router, attn_gain[:, None], moe_gain[:, None], jnp.zeros((share, LANES - E - 2), BF)], axis=1
    )
    own = jnp.concatenate([w_query, w_keyval, w_out, small], axis=1)
    pieces = [own] + [onward(own, s) for s in range(1, outer)]
    sent = jnp.concatenate([w_gateup, w_down], axis=1)
    got = lax.all_to_all(
        sent.reshape(PLANE, OWN, *sent.shape[1:]), PLANE_AXES, split_axis=0, concat_axis=0, tiled=True
    )
    homes = [
        [jnp.concatenate([got[:, e, :share].reshape(-1, D), got[:, e, share:].reshape(-1, D)], axis=0)]
        for e in range(OWN)
    ]
    *pieces, homes[0][0], homes[1][0] = tie(*pieces, homes[0][0], homes[1][0])
    packed = gather(jnp.concatenate(pieces, axis=0), PLANE_AXES)

    def ring(e, count=1):
        for _ in range(count):
            homes[e].append(onward(homes[e][-1]))
        return homes[e][-1]

    hot = jnp.sum((routes[:, :, None] == jnp.arange(LANES, dtype=jnp.int32)[None, None, :]).astype(F32), axis=1)
    cot = jnp.concatenate([cotangent, hot.astype(BF)], axis=1)
    cosine, sine = rope_tables(lengths)

    packed, homes[0][-1] = tie(packed, ring(0, outer - 2))
    cot_0 = after(cot[:MB], homes[0][-1])
    from_x, from_y = across(cot_0, "x"), across(cot_0, "y")
    *saved_0, packed = attention_forward(0, outer, place, lengths, tokens, cot, packed, cosine, sine)
    nm_0, from_x, from_y, homes[0][-1] = tie(saved_0[0], from_x, from_y, ring(0))
    nm_0 = gather(nm_0, PLANE_AXES)
    corner_a, corner_b = across(from_x[: MB // 2], "y"), across(from_y[MB // 2 :], "x")
    packed, corner_a, corner_b, homes[1][-1] = tie(packed, corner_a, corner_b, ring(1, max(outer - 3, 0)))
    cot_same = jnp.concatenate([cot_0, from_x, from_y, corner_a, corner_b], axis=0)
    cot_other = across(cot_same, "c")
    saved_1 = attention_forward(1, outer, place, lengths, tokens, cot, packed, cosine, sine)
    nm_1, cot_other, homes[1][-1] = tie(saved_1[0], cot_other, ring(1))
    nm_1 = gather(nm_1, PLANE_AXES)
    ring(1, outer - len(homes[1]))

    rows = [cot_same, cot_other, nm_0, nm_0]
    partial, *carried_a = experts(0, 0, place, rows, packed, homes[0])
    both_0, *carried_b = experts(0, 1, place, rows, packed, homes[1], partial=[partial])
    rows = [nm_1, nm_1]
    partial, *turns_a = experts(1, 0, place, rows, packed, homes[0], carried_a)
    out_1, same_1, other_1, *turns_b = experts(1, 1, place, rows, packed, homes[1], carried_b, [partial])

    turns = [turns_a, turns_b]
    moved = [turns_a[1], turns_b[1]]

    def pass_on(e, first, last):
        for s in range(first, last):
            moved[e] = onward(moved[e] if s == 1 else plus(turns[e][s], moved[e]))
        return moved[e]

    other_1, moved[0] = tie(other_1, pass_on(0, 1, 2))
    both_0 = scatter_sum(both_0, PLANE_AXES)
    rows_0, *old = attention_backward(0, outer, place, tokens, cot, saved_0, both_0, packed, cosine, sine, None)
    old = old + [saved_0[3], saved_0[0]]
    early = rows_0, pass_on(0, 2, outer - 1)
    moved[1] = after(moved[1], rows_0)
    d_mid_1, (rows_0, moved[0]), _ = sum_to_owners(same_1, other_1, early, rows_0)
    pass_on(1, 1, outer - 2)
    summed_0, out_1 = both_0[:, DMID:], scatter_sum(out_1, PLANE_AXES)
    rows_1, grads, grads_other = attention_backward(1, outer, place, tokens, cot, saved_1, d_mid_1, packed, cosine, sine, old)
    grads, grads_other, moved[0], moved[1], out_1 = tie(
        grads, grads_other, pass_on(0, outer - 1, outer), moved[1], out_1
    )
    out_sums = summed_0, out_1
    output = [(saved[4] + part.astype(F32)).astype(BF) for saved, part in zip((saved_0, saved_1), out_sums)]
    beside = (
        (lambda: pass_on(1, outer - 2, outer - 1), lambda v: moved.__setitem__(1, v)),
        (lambda: pass_on(1, outer - 1, outer), lambda v: moved.__setitem__(1, v)),
    )
    grads = sum_weights(grads, grads_other, beside)
    home = jnp.stack([plus(turns[e][0], moved[e]) for e in range(OWN)])
    up, down = home[:, : PLANE * share], home[:, PLANE * share :]
    home = jnp.concatenate(
        [up.reshape(OWN, PLANE, share, D), down.reshape(OWN, PLANE, share // 2, D)], axis=2
    ).transpose(1, 0, 2, 3)
    home = lax.all_to_all(home, PLANE_AXES, split_axis=0, concat_axis=0, tiled=True)
    home = home.reshape(E, -1, D)
    return (
        jnp.concatenate(output, axis=0),
        jnp.concatenate([rows_0, rows_1], axis=0),
        grads[:, 3 * D + E],
        grads[:, :D],
        grads[:, D : 2 * D],
        grads[:, 2 * D : 3 * D],
        grads[:, 3 * D + E + 1],
        grads[:, 3 * D : 3 * D + E],
        home[:, :share].astype(F32),
        home[:, share:].astype(F32),
    )


def solution(mesh):
    count = mesh.shape["fsdp"]
    inner = Mesh(mesh.devices.reshape(count // PLANE, 2, 2, 2), ALL)
    row, vec, mid = P(ALL, None), P(ALL), P(None, ALL, None)
    return jax.shard_map(
        shards,
        mesh=inner,
        in_specs=(row, row, row, row, vec, row, row, row, vec, row, mid, mid),
        out_specs=(row, row, vec, row, row, row, vec, row, mid, mid),
        check_vma=False,
    )
```

```python
import functools

import jax
import jax.numpy as jnp
from jax import lax
from jax.experimental import pallas as pl
from jax.experimental.pallas import tpu as pltpu
from jax.sharding import Mesh, PartitionSpec as P

D = 1024
HD = 64
FF = 512
E = 16
MB = 256
GROUPS = 8
PLANE = 8
OWN = E // PLANE
LANES = 128
WIDE = 3 * D + LANES
DMID = D + LANES
EPS = 1e-05
NEG = -1e30

BF = jnp.bfloat16
F32 = jnp.float32
PLANE_AXES = ("y", "x", "c")
ALL = ("z", "y", "x", "c")


def dot(a, b, ca=1, cb=0):
    return lax.dot_general(a, b, (((ca,), (cb,)), ((), ())), preferred_element_type=F32)


def mean_rows(v):
    return jnp.sum(v, axis=-1, keepdims=True) * (1.0 / v.shape[-1])


def lane_of(rows):
    return lax.broadcasted_iota(jnp.int32, (rows, LANES), 1)


def turned(t, low):
    return jnp.where(low, pltpu.roll(t, LANES - HD // 2, 1), pltpu.roll(t, HD // 2, 1))


def swap(t):
    return pltpu.roll(t, HD, 1)


def gain_rows(w_ref):
    cols = w_ref[:, 3 * D :].astype(F32).T
    return cols[E : E + 1, :], cols[E + 1 : E + 2, :]


def bias_of(lens_ref, micro):
    row = lax.broadcasted_iota(jnp.int32, (MB, MB), 0)
    col = lax.broadcasted_iota(jnp.int32, (MB, MB), 1)
    start = jnp.zeros((MB, MB), jnp.int32)
    end = jnp.int32(0)
    for s in range(3):
        end = end + lens_ref[micro, s]
        start = jnp.where(row >= end, end, start)
    return jnp.where((col >= start) & (col <= row), 0.0, NEG)


def split_pair(block, half):
    low = lane_of(block.shape[0]) < HD
    other = swap(block)
    here, there = (block, other) if half == 0 else (other, block)
    return jnp.concatenate(
        [jnp.where(low, here, 0.0), jnp.where(low, 0.0, there)], axis=0
    ).astype(BF)


def softmax_pair(score, bias):
    halves = []
    for h in range(2):
        s = score[:, h * MB : (h + 1) * MB] * 0.125 + bias
        e = jnp.exp(s - jnp.max(s, axis=1, keepdims=True))
        halves.append(e * (1.0 / jnp.sum(e, axis=1, keepdims=True)))
    return jnp.concatenate(halves, axis=1)


def attention_forward_kernel(
    micro, outer, place_ref, lens_ref, tok_ref, cot_ref, w_ref, cos_ref, sin_ref,
    nm_ref, q_ref, kv_ref, mixed_ref, resid_ref, weight_ref, *ordering,
):
    if not micro:
        ordered_ref, w_all, sems, out_sem = ordering
        share = D // outer // PLANE
        copies = []
        for p in range(PLANE):
            for s in range(outer):
                z = lax.rem(place_ref[1] + outer - s, outer)
                at = pl.ds(pl.multiple_of((z * PLANE + p) * share, share), share)
                block = w_ref.at[(p * outer + s) * share : (p * outer + s + 1) * share]
                copies.append(pltpu.make_async_copy(block, w_all.at[at], sems.at[p * outer + s]))
        for copy in copies:
            copy.start()
        for copy in copies:
            copy.wait()
        write = pltpu.make_async_copy(w_all, ordered_ref, out_sem)
        write.start()
        w_ref = w_all
    gain_in, gain_mid = gain_rows(w_ref)
    x = tok_ref[...].astype(F32)
    normed = (x * lax.rsqrt(mean_rows(x * x) + EPS) * gain_in).astype(BF)
    q_lin = dot(normed, w_ref[:, :D])
    kv_lin = dot(normed, w_ref[:, D : 2 * D])
    cosine, sine = cos_ref[...], sin_ref[...]
    low = (lane_of(MB) % HD) < HD // 2
    bias = bias_of(lens_ref, micro)
    mixed = []
    for pair in range(GROUPS // 2):
        lanes = slice(pair * LANES, (pair + 1) * LANES)
        k_pair = kv_lin[:, lanes]
        k_pair = k_pair * cosine + turned(k_pair, low) * sine
        v_pair = kv_lin[:, D // 2 + pair * LANES : D // 2 + (pair + 1) * LANES]
        kv_ref[:, lanes] = k_pair.astype(BF)
        kv_ref[:, D // 2 + pair * LANES : D // 2 + (pair + 1) * LANES] = v_pair.astype(BF)
        for half in range(2):
            group = 2 * pair + half
            q = q_lin[:, group * LANES : (group + 1) * LANES]
            q = (q * cosine + turned(q, low) * sine).astype(BF)
            q_ref[:, group * LANES : (group + 1) * LANES] = q
            score = dot(q, split_pair(k_pair, half), 1, 1)
            weight = softmax_pair(score, bias).astype(BF)
            weight_ref[:, group * 2 * MB : (group + 1) * 2 * MB] = weight
            mixed.append(dot(weight, split_pair(v_pair, half)).astype(BF))
    mixed = jnp.concatenate(mixed, axis=1)
    mixed_ref[...] = mixed
    resid = x + dot(mixed, w_ref[:, 2 * D : 3 * D])
    resid_ref[...] = resid
    nm_ref[:, -D:] = (resid * lax.rsqrt(mean_rows(resid * resid) + EPS) * gain_mid).astype(BF)
    if micro:
        nm_ref[:, :DMID] = cot_ref[...]
    else:
        write.wait()


def masked_gates(logits, routed):
    top = jnp.max(jnp.where(routed, logits, NEG), axis=1, keepdims=True)
    e = jnp.where(routed, jnp.exp(jnp.minimum(logits - top, 0.0)), 0.0)
    return e * (1.0 / jnp.sum(e, axis=1, keepdims=True))


def plane_back(place_ref, s, outer, rows):
    z = lax.rem(place_ref[1] + outer - s, outer)
    return pl.ds(pl.multiple_of(z * rows, rows), rows)


def expert_kernel(outer, micro, e, *refs):
    refs = list(refs)
    take = lambda k: [refs.pop(0) for _ in range(k)]
    place_ref, *peers = take(3 if micro else 5)
    wr_ref = take(1)[0]
    homes = take(outer)
    partial_ref = take(1)[0] if e else None
    carried = take(2) if micro else []
    out_ref = take(1)[0]
    dmid_refs = take(2) if micro and e else []
    grads = take(outer) if micro else []
    acc_gu, acc_dn, w_gu, w_dn, sems = take(5)
    old_gu, old_dn = take(2) if micro else (None, None)
    step = pl.program_id(0)
    up_rows, down_rows = D // outer, FF // outer

    def old_copies():
        return [
            pltpu.make_async_copy(source, target, sems.at[outer, k])
            for k, (source, target) in enumerate(zip(carried, (old_gu, old_dn)))
        ]

    @pl.when(step == 0)
    def _():
        copies = []
        for s in range(outer):
            copies += [
                pltpu.make_async_copy(
                    homes[s].at[:up_rows], w_gu.at[plane_back(place_ref, s, outer, up_rows)], sems.at[s, 0]
                ),
                pltpu.make_async_copy(
                    homes[s].at[up_rows:], w_dn.at[plane_back(place_ref, s, outer, down_rows)], sems.at[s, 1]
                ),
            ]
        for copy in copies + (old_copies() if micro else []):
            copy.start()
        acc_gu[...] = jnp.zeros_like(acc_gu)
        acc_dn[...] = jnp.zeros_like(acc_dn)
        for copy in copies:
            copy.wait()

    cots, nms = (peers, peers) if micro else (peers[:2], peers[2:])
    nm = jnp.concatenate([ref[:, -D:] for ref in nms], axis=0)
    cot = jnp.concatenate([ref[:, :D] for ref in cots], axis=0)
    hot = jnp.concatenate([ref[:, D:DMID] for ref in cots], axis=0).astype(F32)
    lane = lane_of(nm.shape[0])
    expert = place_ref[0] * OWN + e
    if e:
        handed = partial_ref[:, D:DMID].astype(F32)
        mine = (lane == expert + 2 * E) | (lane == expert + 3 * E)
        combine = jnp.sum(jnp.where(mine, handed, 0.0), axis=1, keepdims=True)
    else:
        gates = masked_gates(dot(nm, wr_ref[...]), hot > 0.5)
        combine = jnp.sum(jnp.where(lane == expert, gates, 0.0), axis=1, keepdims=True)
    gateup = dot(nm, w_gu[...])
    gate, up = gateup[:, :FF], gateup[:, FF:]
    s = 1.0 / (1.0 + jnp.exp(-gate))
    silu = gate * s
    act = silu * up
    d_plain = dot(cot, w_dn[...], 1, 1)
    d_combine = jnp.sum(act * d_plain, axis=1, keepdims=True)
    act = (act * combine).astype(BF)
    out = dot(act, w_dn[...])
    d_act = d_plain * combine
    d_gateup = jnp.concatenate(
        [(d_act * up * (s * (1.0 + gate * (1.0 - s)))).astype(BF), (d_act * silu).astype(BF)], axis=1
    )
    d_mid = dot(d_gateup, w_gu[...], 1, 1)
    acc_gu[...] += dot(nm, d_gateup, 0, 0)
    acc_dn[...] += dot(act, cot, 0, 0)
    high = d_combine.astype(BF).astype(F32)
    extra = jnp.where(lane == expert, high, 0.0) + jnp.where(lane == expert + E, d_combine - high, 0.0)
    if e:
        d_mid = d_mid + partial_ref[:, :D].astype(F32)
        extra = extra + jnp.where(lane < 2 * E, handed, 0.0)
        out = out + partial_ref[:, DMID:].astype(F32)
    else:
        high = gates.astype(BF).astype(F32)
        extra = extra + pltpu.roll(high, 2 * E, 1) + pltpu.roll(gates - high, 3 * E, 1)
    d_mid = jnp.concatenate([d_mid.astype(BF), extra.astype(BF)], axis=1)
    out = out.astype(BF)
    if not e:
        out_ref[:, :DMID] = d_mid
        out_ref[:, DMID:] = out
    else:
        core = lax.rem(place_ref[0], 2)
        for half in range(2):
            part = slice(half * MB, (half + 1) * MB)
            at = pl.ds(pl.multiple_of((core if half == 0 else 1 - core) * MB, MB), MB)
            if micro:
                out_ref[at, :] = out[part]
                dmid_refs[half][...] = d_mid[part]
            else:
                out_ref[at, :DMID] = d_mid[part]
                out_ref[at, DMID:] = out[part]

    if micro:

        @pl.when(step == pl.num_programs(0) - 1)
        def _():
            for copy in old_copies():
                copy.wait()
            for s in range(outer):
                at = plane_back(place_ref, s, outer, up_rows)
                grads[s][:up_rows] = (acc_gu[at] + old_gu[at]).astype(BF)
                at = plane_back(place_ref, s, outer, down_rows)
                grads[s][up_rows:] = (acc_dn[at] + old_dn[at]).astype(BF)


def join_pair(a0, b0, a1, b1, low):
    return jnp.where(low, a0, b1) + swap(jnp.where(low, a1, b0))


def attention_backward_kernel(outer, last, *refs):
    refs = list(refs)
    take = lambda k: [refs.pop(0) for _ in range(k)]
    place_ref = take(1)[0]
    (tok_ref, cot_ref, nm_ref, q_ref, kv_ref, mixed_ref, resid_ref, weight_ref, dmid_ref, w_ref, cos_ref, sin_ref) = take(12)
    old = take(8) if last else []
    rows_ref = take(1)[0]
    kept = take(2 if last else 6)
    gain_in, gain_mid = gain_rows(w_ref)
    lane = lane_of(MB)
    cot = cot_ref[:, :D].astype(F32)
    resid = resid_ref[...]
    nm = nm_ref[:, -D:]
    w_small = w_ref[:, 3 * D :]
    gates = masked_gates(dot(nm, w_small), cot_ref[:, D:].astype(F32) > 0.5)
    pieces = dmid_ref[:, D:].astype(F32)
    d_gates = pieces + pltpu.roll(pieces, LANES - E, 1)
    d_logits = gates * (d_gates - jnp.sum(gates * d_gates, axis=1, keepdims=True))
    d_logits = jnp.where(lane < E, d_logits, 0.0).astype(BF)
    d_mid = dmid_ref[:, :D].astype(F32) + dot(d_logits, w_small, 1, 1)
    inverse = lax.rsqrt(mean_rows(resid * resid) + EPS)
    u = d_mid * gain_mid
    d_resid = cot + inverse * u - resid * (inverse * inverse * inverse) * mean_rows(u * resid)
    gain_mid_grad = jnp.sum(d_mid * resid * inverse, axis=0, keepdims=True)
    d_branch = d_resid.astype(BF)
    both = lambda k, value: jnp.concatenate([old[k][...], value], axis=0)
    leaving = []

    def leave(k, part):
        grad_ref, sems = refs
        share = D // outer // PLANE
        for s in range(outer):
            z = lax.rem(place_ref[1] + s, outer)
            for q in range(PLANE // 2):
                for other in range(2):
                    device = lax.bitwise_xor(place_ref[0], 2 * q + other)
                    at = pl.ds(pl.multiple_of((z * PLANE + device) * share, share), share)
                    sem = sems.at[k, s * PLANE + 2 * q + other]
                    copy = pltpu.make_async_copy(grad_ref.at[at, part], kept[other].at[s, q, :, part], sem)
                    copy.start()
                    leaving.append(copy)

    if last:
        refs[0][:, 2 * D : 3 * D] = dot(both(6, mixed_ref[...]), both(3, d_branch), 0, 0).astype(BF)
        leave(0, slice(2 * D, 3 * D))
    d_mixed = dot(d_branch, w_ref[:, 2 * D : 3 * D], 1, 1).astype(BF)

    cosine, sine = cos_ref[...], sin_ref[...]
    low = (lane % HD) < HD // 2
    head_low = lane < HD
    d_q, d_k, d_v = [], [], []
    for pair in range(GROUPS // 2):
        k_pair = kv_ref[:, pair * LANES : (pair + 1) * LANES].astype(F32)
        v_pair = kv_ref[:, D // 2 + pair * LANES : D // 2 + (pair + 1) * LANES].astype(F32)
        keys, values = [], []
        for half in range(2):
            group = 2 * pair + half
            q = q_ref[:, group * LANES : (group + 1) * LANES]
            dm = d_mixed[:, group * LANES : (group + 1) * LANES]
            k_two = split_pair(k_pair, half)
            weight = weight_ref[:, group * 2 * MB : (group + 1) * 2 * MB]
            p = weight.astype(F32)
            d_weight = dot(dm, split_pair(v_pair, half), 1, 1)
            scored = p * d_weight
            d_score = []
            for h in range(2):
                part = slice(h * MB, (h + 1) * MB)
                total = jnp.sum(scored[:, part], axis=1, keepdims=True)
                d_score.append((p[:, part] * (d_weight[:, part] - total)).astype(BF))
            d_score = jnp.concatenate(d_score, axis=1)
            d_query = dot(d_score, k_two) * 0.125
            d_q.append((d_query * cosine - turned(d_query, low) * sine).astype(BF))
            d_key = dot(d_score, q, 0, 0) * 0.125
            d_value = dot(weight, dm, 0, 0)
            keys += [d_key[:MB], d_key[MB:]]
            values += [d_value[:MB], d_value[MB:]]
        d_key = join_pair(*keys, head_low)
        d_k.append((d_key * cosine - turned(d_key, low) * sine).astype(BF))
        d_v.append(join_pair(*values, head_low).astype(BF))
    d_q = jnp.concatenate(d_q, axis=1)
    d_kv = jnp.concatenate(d_k + d_v, axis=1)

    x = tok_ref[...].astype(F32)
    inverse = lax.rsqrt(mean_rows(x * x) + EPS)
    normed = (x * inverse * gain_in).astype(BF)
    if last:
        normed_two = both(0, normed)
        refs[0][:, : D] = dot(normed_two, both(1, d_q), 0, 0).astype(BF)
        refs[0][:, D : 2 * D] = dot(normed_two, both(2, d_kv), 0, 0).astype(BF)
        leave(1, slice(0, 2 * D))
    d_in = dot(d_q, w_ref[:, :D], 1, 1) + dot(d_kv, w_ref[:, D : 2 * D], 1, 1)
    v = d_in * gain_in
    rows_ref[...] = d_resid + inverse * v - x * (inverse * inverse * inverse) * mean_rows(v * x)
    gain_in_grad = jnp.sum(d_in * x * inverse, axis=0, keepdims=True)
    gains = jnp.concatenate([gain_in_grad, gain_mid_grad, jnp.zeros((6, D), F32)], axis=0)
    if not last:
        for ref, value in zip(kept, (normed, d_q, d_kv, d_branch, d_logits, gains)):
            ref[...] = value
        return
    gains = jnp.concatenate([jnp.zeros((E, D), F32), gains + old[5][...], jnp.zeros((LANES - E - 8, D), F32)], axis=0)
    refs[0][:, 3 * D :] = (dot(both(7, nm), both(4, d_logits), 0, 0) + gains.T).astype(BF)
    leave(2, slice(3 * D, WIDE))
    for copy in leaving:
        copy.wait()


def blk(shape, index, buffers=None):
    if buffers is None:
        return pl.BlockSpec(shape, index)
    return pl.BlockSpec(shape, index, pipeline_mode=pl.Buffered(buffers))


def kernel_params(mib=58):
    return pltpu.CompilerParams(dimension_semantics=("arbitrary",), vmem_limit_bytes=mib << 20)


def takes(us):
    return pl.CostEstimate(flops=int(us * 1.15e9), bytes_accessed=1 << 20, transcendentals=0)


def shaped(rows, width, kind=BF):
    return jax.ShapeDtypeStruct((rows, width), kind)


def own_rows(width, micro=0):
    return blk((MB, width), lambda i, *_: (micro, 0))


def whole(shape):
    return blk(shape, lambda i, *_: (0,) * len(shape), 1)


def attention_forward(micro, outer, place, lengths, tokens, cot, packed, cosine, sine):
    width = DMID + D if micro else D
    any_ref = pl.BlockSpec(memory_space=pl.ANY)
    return pl.pallas_call(
        functools.partial(attention_forward_kernel, micro, outer),
        grid_spec=pltpu.PrefetchScalarGridSpec(
            num_scalar_prefetch=2,
            grid=(1,),
            in_specs=[own_rows(D, micro), own_rows(DMID, micro), whole((D, WIDE)) if micro else any_ref]
            + [own_rows(LANES, micro)] * 2,
            out_specs=[own_rows(width)] + [own_rows(D)] * 4 + [own_rows(D * 4)] + ([] if micro else [any_ref]),
            scratch_shapes=[]
            if micro
            else [pltpu.VMEM((D, WIDE), BF), pltpu.SemaphoreType.DMA((PLANE * outer,)), pltpu.SemaphoreType.DMA],
        ),
        out_shape=[shaped(MB, width)]
        + [shaped(MB, D)] * 3
        + [shaped(MB, D, F32), shaped(MB, D * 4)]
        + ([] if micro else [shaped(D, WIDE)]),
        compiler_params=kernel_params(),
        cost_estimate=takes(12),
        name=f"attention_forward_{micro}",
    )(place, lengths, tokens, cot, packed, cosine, sine)


def experts(micro, e, place, rows, packed, homes, carried=(), partial=()):
    outer = len(homes)
    wide = DMID + D
    any_ref = pl.BlockSpec(memory_space=pl.ANY)
    shape = jax.ShapeDtypeStruct

    def peer(k, width):
        return blk((MB, width), lambda i, place, *_: (lax.bitwise_xor(place[0], 2 * i + k), 0))

    near = blk((MB, DMID), lambda i, *_: (i, 0))
    pair = blk((2 * MB, wide), lambda i, *_: (i, 0))
    home = shape(homes[0].shape, BF)
    acc = [shape((D, 2 * FF), F32), shape((FF, D), F32)]
    in_specs = [peer(0, wide), peer(1, wide)] if micro else [near, near, peer(0, D), peer(1, D)]
    in_specs += [blk((D, LANES), lambda i, *_: (0, 3 * D // LANES), 1)]
    in_specs += [any_ref] * outer + [pair] * len(partial) + [any_ref] * len(carried)
    scratch = [
        pltpu.VMEM((D, 2 * FF), BF),
        pltpu.VMEM((FF, D), BF),
        pltpu.SemaphoreType.DMA((outer + 1, 2)),
    ]
    if not e:
        out_specs, out_shape = [pair], [shaped(PLANE * MB, wide)]
    else:
        width = D if micro else wide
        out_specs = [blk((2 * MB, width), lambda i, place, *_: (lax.bitwise_xor(place[0] // 2, i), 0))]
        out_shape = [shaped(PLANE * MB, width)]
        if micro:
            out_specs += [near, near]
            out_shape += [shaped(PLANE // 2 * MB, DMID)] * 2
    if micro:
        out_specs += [whole(home.shape)] * outer
        out_shape += [home] * outer
        scratch = [pltpu.VMEM(a.shape, F32) for a in acc] + scratch + [pltpu.VMEM(a.shape, F32) for a in acc]
    else:
        out_specs += [whole(a.shape) for a in acc]
        out_shape += acc
    return pl.pallas_call(
        functools.partial(expert_kernel, outer, micro, e),
        grid_spec=pltpu.PrefetchScalarGridSpec(
            num_scalar_prefetch=1,
            grid=(PLANE // 2,),
            in_specs=in_specs,
            out_specs=out_specs,
            scratch_shapes=scratch,
        ),
        out_shape=out_shape,
        compiler_params=kernel_params(48 if not micro and not e else 58),
        cost_estimate=takes(28),
        name=f"experts_{micro}_{e}",
    )(place, *rows, packed, *homes, *partial, *carried)


def attention_backward(micro, outer, place, tokens, cot, saved, d_mid, packed, cosine, sine, old):
    last = old is not None
    any_ref = pl.BlockSpec(memory_space=pl.ANY)
    in_specs = [own_rows(D, micro), own_rows(DMID, micro)] + [own_rows(v.shape[1]) for v in saved]
    in_specs += [own_rows(DMID), whole((D, WIDE)), own_rows(LANES, micro), own_rows(LANES, micro)]
    args = [tokens, cot, *saved, d_mid, packed, cosine, sine]
    kept = [shaped(MB, D)] * 4 + [shaped(MB, LANES), shaped(8, D, F32)]
    kept_specs = [whole(a.shape) for a in kept]
    scratch = []
    if last:
        args += old
        in_specs += [whole(a.shape) for a in old]
        share = D // outer // PLANE
        kept = [jax.ShapeDtypeStruct((outer, PLANE // 2, share, WIDE), BF)] * 2
        kept_specs = [any_ref] * 2
        scratch = [pltpu.VMEM((D, WIDE), BF), pltpu.SemaphoreType.DMA((3, outer * PLANE))]
    return pl.pallas_call(
        functools.partial(attention_backward_kernel, outer, last),
        grid_spec=pltpu.PrefetchScalarGridSpec(
            num_scalar_prefetch=1,
            grid=(1,),
            in_specs=in_specs,
            out_specs=[own_rows(D)] + kept_specs,
            scratch_shapes=scratch,
        ),
        out_shape=[shaped(MB, D, F32)] + kept,
        compiler_params=kernel_params(50 if last else 58),
        cost_estimate=takes(18 if last else 13),
        name=f"attention_backward_{micro}",
    )(place, *args)


def rope_tables(lengths):
    ends = jnp.stack([jnp.sum(lengths[:, : s + 1], axis=1) for s in range(lengths.shape[1] - 1)], axis=1)
    index = jnp.arange(MB, dtype=jnp.int32)
    start = jnp.max(jnp.where(ends[:, None, :] <= index[None, :, None], ends[:, None, :], 0), axis=2)
    position = (index[None, :] - start).astype(F32).reshape(-1)
    lane = jnp.arange(LANES, dtype=jnp.int32)
    freq = jnp.exp(-((2 * (lane % (HD // 2))).astype(F32) / HD) * jnp.log(10000.0))
    angle = position[:, None] * freq[None, :]
    sign = jnp.where(lane % HD < HD // 2, -1.0, 1.0)
    return jnp.cos(angle), jnp.sin(angle) * sign[None, :]


def gather(v, axes):
    return lax.all_gather(v, axes, axis=0, tiled=True)


def scatter_sum(v, axes, dim=0):
    return lax.psum_scatter(v, axes, scatter_dimension=dim, tiled=True)


def tie(*values):
    return lax.optimization_barrier(values)


def after(v, *others):
    return tie(v, *others)[0]


def across(v, axis):
    return lax.ppermute(v, axis, [(0, 1), (1, 0)])


def onward(v, steps=1):
    count = lax.axis_size("z")
    return lax.ppermute(v, "z", [(i, (i + steps) % count) for i in range(count)])


def plus(a, b):
    return (a.astype(F32) + b.astype(F32)).astype(BF)


def sum_weights(same, other, beside):
    outer = same.shape[0]
    cut = same.shape[-1] // 2 // LANES * LANES

    def both(stage, *values):
        start, took = beside[stage]
        *values, extra = tie(*values, start())
        took(extra)
        return values

    total = plus(same, across(other, "c"))
    first, second = total[..., :cut], total[..., cut:]
    got_x, got_y = both(0, across(first[:, 1::2], "x"), across(second[:, 2:], "y"))
    first, second = plus(first[:, ::2], got_x), plus(second[:, :2], got_y)
    beside[1][1](beside[1][0]())
    got_y, got_x = across(first[:, 1], "y"), across(second[:, 1], "x")
    total = jnp.concatenate([plus(first[:, 0], got_y), plus(second[:, 0], got_x)], axis=-1)
    terms = [total[0]] + [onward(total[s], s) for s in range(1, outer)]
    return sum(term.astype(F32) for term in terms)


def sum_to_owners(same, other, early, late):
    total = plus(same, across(other, "c"))
    total = total.reshape(4, 2, MB // 2, -1)
    first = [total[i, 0] for i in range(4)]
    second = [total[i, 1] for i in range(4)]
    got_x = across(jnp.stack([first[1], first[3]]), "x")
    got_y = across(jnp.stack([second[2], second[3]]), "y")
    got_x, got_y, early = tie(got_x, got_y, early)
    last_x, last_y = across(plus(second[1], got_y[1]), "x"), across(plus(first[2], got_x[1]), "y")
    last_x, last_y, late = tie(last_x, last_y, late)
    return jnp.concatenate(
        [
            (first[0].astype(F32) + got_x[0].astype(F32) + last_y.astype(F32)).astype(BF),
            (second[0].astype(F32) + got_y[0].astype(F32) + last_x.astype(F32)).astype(BF),
        ],
        axis=0,
    ), early, late


def shards(tokens, cotangent, lengths, routes, attn_gain, w_query, w_keyval, w_out, moe_gain, w_router, w_gateup, w_down):
    share = w_query.shape[0]
    outer = lax.axis_size("z")
    place = jnp.stack([lax.axis_index(PLANE_AXES), lax.axis_index("z")]).astype(jnp.int32)

    small = jnp.concatenate(
        [w_router, attn_gain[:, None], moe_gain[:, None], jnp.zeros((share, LANES - E - 2), BF)], axis=1
    )
    own = jnp.concatenate([w_query, w_keyval, w_out, small], axis=1)
    pieces = [own] + [onward(own, s) for s in range(1, outer)]
    sent = jnp.concatenate([w_gateup, w_down], axis=1)
    got = lax.all_to_all(
        sent.reshape(PLANE, OWN, *sent.shape[1:]), PLANE_AXES, split_axis=0, concat_axis=0, tiled=True
    )
    homes = [
        [jnp.concatenate([got[:, e, :share].reshape(-1, D), got[:, e, share:].reshape(-1, D)], axis=0)]
        for e in range(OWN)
    ]
    *pieces, homes[0][0], homes[1][0] = tie(*pieces, homes[0][0], homes[1][0])
    packed = gather(jnp.concatenate(pieces, axis=0), PLANE_AXES)

    def ring(e, count=1):
        for _ in range(count):
            homes[e].append(onward(homes[e][-1]))
        return homes[e][-1]

    hot = jnp.sum((routes[:, :, None] == jnp.arange(LANES, dtype=jnp.int32)[None, None, :]).astype(F32), axis=1)
    cot = jnp.concatenate([cotangent, hot.astype(BF)], axis=1)
    cosine, sine = rope_tables(lengths)

    packed, homes[0][-1] = tie(packed, ring(0, outer - 2))
    cot_0 = after(cot[:MB], homes[0][-1])
    from_x, from_y = across(cot_0, "x"), across(cot_0, "y")
    *saved_0, packed = attention_forward(0, outer, place, lengths, tokens, cot, packed, cosine, sine)
    nm_0, from_x, from_y, homes[0][-1] = tie(saved_0[0], from_x, from_y, ring(0))
    nm_0 = gather(nm_0, PLANE_AXES)
    corner_a, corner_b = across(from_x[: MB // 2], "y"), across(from_y[MB // 2 :], "x")
    packed, corner_a, corner_b, homes[1][-1] = tie(packed, corner_a, corner_b, ring(1, max(outer - 3, 0)))
    cot_same = jnp.concatenate([cot_0, from_x, from_y, corner_a, corner_b], axis=0)
    cot_other = across(cot_same, "c")
    saved_1 = attention_forward(1, outer, place, lengths, tokens, cot, packed, cosine, sine)
    nm_1, cot_other, homes[1][-1] = tie(saved_1[0], cot_other, ring(1))
    nm_1 = gather(nm_1, PLANE_AXES)
    ring(1, outer - len(homes[1]))

    rows = [cot_same, cot_other, nm_0, nm_0]
    partial, *carried_a = experts(0, 0, place, rows, packed, homes[0])
    both_0, *carried_b = experts(0, 1, place, rows, packed, homes[1], partial=[partial])
    rows = [nm_1, nm_1]
    partial, *turns_a = experts(1, 0, place, rows, packed, homes[0], carried_a)
    out_1, same_1, other_1, *turns_b = experts(1, 1, place, rows, packed, homes[1], carried_b, [partial])

    turns = [turns_a, turns_b]
    moved = [turns_a[1], turns_b[1]]

    def pass_on(e, first, last):
        for s in range(first, last):
            moved[e] = onward(moved[e] if s == 1 else plus(turns[e][s], moved[e]))
        return moved[e]

    other_1, moved[0] = tie(other_1, pass_on(0, 1, 2))
    both_0 = scatter_sum(both_0, PLANE_AXES)
    rows_0, *old = attention_backward(0, outer, place, tokens, cot, saved_0, both_0, packed, cosine, sine, None)
    old = old + [saved_0[3], saved_0[0]]
    early = rows_0, pass_on(0, 2, outer - 1)
    moved[1] = after(moved[1], rows_0)
    d_mid_1, (rows_0, moved[0]), _ = sum_to_owners(same_1, other_1, early, rows_0)
    pass_on(1, 1, outer - 2)
    summed_0, out_1 = both_0[:, DMID:], scatter_sum(out_1, PLANE_AXES)
    rows_1, grads, grads_other = attention_backward(1, outer, place, tokens, cot, saved_1, d_mid_1, packed, cosine, sine, old)
    grads, grads_other, moved[0], moved[1], out_1 = tie(
        grads, grads_other, pass_on(0, outer - 1, outer), moved[1], out_1
    )
    out_sums = summed_0, out_1
    output = [(saved[4] + part.astype(F32)).astype(BF) for saved, part in zip((saved_0, saved_1), out_sums)]
    beside = (
        (lambda: pass_on(1, outer - 2, outer - 1), lambda v: moved.__setitem__(1, v)),
        (lambda: pass_on(1, outer - 1, outer), lambda v: moved.__setitem__(1, v)),
    )
    grads = sum_weights(grads, grads_other, beside)
    home = jnp.stack([plus(turns[e][0], moved[e]) for e in range(OWN)])
    up, down = home[:, : PLANE * share], home[:, PLANE * share :]
    home = jnp.concatenate(
        [up.reshape(OWN, PLANE, share, D), down.reshape(OWN, PLANE, share // 2, D)], axis=2
    ).transpose(1, 0, 2, 3)
    home = lax.all_to_all(home, PLANE_AXES, split_axis=0, concat_axis=0, tiled=True)
    home = home.reshape(E, -1, D)
    return (
        jnp.concatenate(output, axis=0),
        jnp.concatenate([rows_0, rows_1], axis=0),
        grads[:, 3 * D + E],
        grads[:, :D],
        grads[:, D : 2 * D],
        grads[:, 2 * D : 3 * D],
        grads[:, 3 * D + E + 1],
        grads[:, 3 * D : 3 * D + E],
        home[:, :share].astype(F32),
        home[:, share:].astype(F32),
    )


def solution(mesh):
    count = mesh.shape["fsdp"]
    inner = Mesh(mesh.devices.reshape(count // PLANE, 2, 2, 2), ALL)
    row, vec, mid = P(ALL, None), P(ALL), P(None, ALL, None)
    return jax.shard_map(
        shards,
        mesh=inner,
        in_specs=(row, row, row, row, vec, row, row, row, vec, row, mid, mid),
        out_specs=(row, row, vec, row, row, row, vec, row, mid, mid),
        check_vma=False,
    )
```
